32 devices in a mesh: gx: 8 (over y, x, core), gy: 4 (over z).
Axes of the slice: x: 2, y: 2, z: 4, core: 2. Of those that a mesh axis runs over, the one named last changes fastest.
Arguments:
- leaf_maps: float32 [8, 4, 1024, 1024], P('gx', 'gy'), may hold values from -8 to 40, as said below
- edge_data: float32 [8, 4, 512, 1024], P('gx', 'gy'), may hold values from -6 to 6
Outputs:
- potential: float32 [8, 4, 1024, 1024], P('gx', 'gy')
- flux: float32 [8, 4, 1024, 1024], P('gx', 'gy')
The draws below stay inside these ranges and needn't reach their ends.
Inputs may be any that keep to these rules, and one draw needn't show every extreme that they name: `leaf_maps`: each leaf's map is exactly symmetric and positive definite.
All inputs are finite; a program needn't handle non-finite values.
Results may differ from the reference program's by a relative error of at most 0.0003.
Values sent between devices are 32-bit elements; how exact they have to be, the bound alone decides.
No kernel may reach another device: no remote copies, remote signals or barrier semaphores. Data moves between devices by JAX's collectives and lax.ppermute only.
A program may use at most 128 MiB of HBM per device.

```python
import math
import jax
import jax.numpy as jnp
from jax import lax

EDGE = 256
RHS_COUNT = 1024
BOX_COLS = 8
BOX_ROWS = 4


def draw_leaf_maps(key, part):
    full_len = 4 * EDGE
    shared = jax.random.fold_in(key, 101)
    raw = jax.random.normal(jax.random.fold_in(shared, 1), (EDGE, EDGE), jnp.float32)
    basis, upper = jnp.linalg.qr(raw)
    signs = jnp.where(jnp.diagonal(upper) < 0, -1.0, 1.0).astype(jnp.float32)
    basis = basis * signs[None, :]
    spectrum = jnp.exp(jax.random.uniform(jax.random.fold_in(shared, 2), (EDGE,), jnp.float32, math.log(0.01), 0.0))

    def single_map(sub_key):
        values = jax.random.normal(sub_key, (full_len, full_len), jnp.float32)
        mixing = jnp.dot(values, values.T, precision=lax.Precision.HIGHEST) / full_len + 0.5 * jnp.eye(full_len, dtype=jnp.float32)
        mixing = 0.5 * (mixing + mixing.T)
        factors = jnp.exp(jax.random.uniform(jax.random.fold_in(sub_key, 3), (4, EDGE), jnp.float32, 0.0, math.log(2.0)))
        roots = jnp.sqrt(spectrum[None, :] * factors).reshape(full_len)
        inner = (roots[:, None] * mixing * roots[None, :]).reshape(4, EDGE, 4, EDGE)
        rotated = jnp.einsum('ia,xaye,je->xiyj', basis, inner, basis, precision=lax.Precision.HIGHEST)
        matrix = rotated.reshape(full_len, full_len)
        return 0.5 * (matrix + matrix.T)
    sub_keys = jax.random.split(key, BOX_COLS * BOX_ROWS)
    maps = lax.map(single_map, sub_keys)
    return maps.reshape(BOX_COLS, BOX_ROWS, full_len, full_len)


def levels(stream_key, shape, cuts, least, high):
    def one(dim, blocks):
        heights = jax.random.uniform(jax.random.fold_in(jax.random.fold_in(stream_key, 6), dim), (blocks,), jnp.float32, least / len(cuts), high / len(cuts))
        return jnp.repeat(jnp.exp(heights), shape[dim] // blocks).reshape((-1,) + (1,) * (len(shape) - dim - 1))

    loudness = one(*cuts[0])
    for cut in cuts[1:]:
        loudness = loudness * one(*cut)
    return loudness


def normal_values(own_key, dims, spread, limit, cuts=(), kind=jnp.bfloat16):
    level = levels(own_key, dims, cuts, -0.22, 0.18) if cuts else 1.0
    entries = jax.random.normal(own_key, dims, jnp.float32) * spread * level
    return jnp.minimum(jnp.maximum(entries, -limit), limit).astype(kind)


def setup_inputs(seed: int = 0) -> dict:
    key_list = jax.random.split(jax.random.key(seed), 3)
    leaf_maps = draw_leaf_maps(jax.random.fold_in(key_list[2], 71), 0)
    edge_data = normal_values(key_list[1], (BOX_COLS, BOX_ROWS, 2 * EDGE, RHS_COUNT), 1.0, 6.0, ((0, 8), (1, 4)), jnp.float32)
    return dict(leaf_maps=leaf_maps, edge_data=edge_data)


def product(left, right):
    return jnp.dot(left.astype(jnp.float32), right.astype(jnp.float32), precision=lax.Precision.HIGHEST, preferred_element_type=jnp.float32)

def solve_definite(matrix, values):
    return jax.scipy.linalg.cho_solve((jnp.linalg.cholesky(matrix), True), values)

def group_solve(inputs):
    blocks, data = inputs
    edge_len = blocks.shape[-1] // 4
    zero_half = jnp.zeros((edge_len, 3 * edge_len), jnp.float32)

    def outside(block, start):
        return jnp.concatenate([block[:, start:start + edge_len], block[:, 2 * edge_len:]], 1)
    zmats = []
    mparts = {}
    rparts = {}
    for row_bit in range(2):
        left_map, right_map = (blocks[0, row_bit], blocks[1, row_bit])
        m_first = left_map[edge_len:2 * edge_len, edge_len:2 * edge_len] + right_map[:edge_len, :edge_len]
        bmat = jnp.concatenate([outside(left_map[edge_len:2 * edge_len], 0), outside(right_map[:edge_len], edge_len)], 1)
        zmat = solve_definite(m_first, bmat)
        zmats.append(zmat)
        y_start = 3 * edge_len - edge_len * row_bit
        prows = [jnp.concatenate([outside(left_map[y_start:y_start + edge_len], 0), zero_half], 1) - product(left_map[y_start:y_start + edge_len, edge_len:2 * edge_len], zmat), jnp.concatenate([zero_half, outside(right_map[y_start:y_start + edge_len], edge_len)], 1) - product(right_map[y_start:y_start + edge_len, :edge_len], zmat)]
        data_left, data_right = (data[0, row_bit], data[1, row_bit])
        for col_bit in range(2):
            half_left = prows[col_bit][:, :3 * edge_len]
            half_right = prows[col_bit][:, 3 * edge_len:]
            y_col = edge_len + edge_len * row_bit
            i_col = 2 * edge_len - edge_len * row_bit
            rparts[col_bit, row_bit] = product(half_left[:, :edge_len], data_left[:edge_len]) + product(half_left[:, y_col:y_col + edge_len], data_left[edge_len:]) + product(half_right[:, :edge_len], data_right[:edge_len]) + product(half_right[:, y_col:y_col + edge_len], data_right[edge_len:])
            mparts[col_bit, row_bit] = jnp.concatenate([half_left[:, i_col:i_col + edge_len], half_right[:, i_col:i_col + edge_len]], 1)
    m_second = jnp.concatenate([mparts[0, 0] + mparts[0, 1], mparts[1, 0] + mparts[1, 1]], 0)
    rhs = jnp.concatenate([rparts[0, 0] + rparts[0, 1], rparts[1, 0] + rparts[1, 1]], 0)
    top = -solve_definite(m_second, rhs)
    top_left, top_right = (top[:edge_len], top[edge_len:])
    potentials = [[None, None], [None, None]]
    fluxes = [[None, None], [None, None]]
    for row_bit in range(2):
        data_left, data_right = (data[0, row_bit], data[1, row_bit])
        if row_bit == 0:
            south_left, north_left = (data_left[edge_len:], top_left)
            south_right, north_right = (data_right[edge_len:], top_right)
        else:
            south_left, north_left = (top_left, data_left[edge_len:])
            south_right, north_right = (top_right, data_right[edge_len:])
        uext = jnp.concatenate([data_left[:edge_len], south_left, north_left, data_right[:edge_len], south_right, north_right], 0)
        middle = -product(zmats[row_bit], uext)
        pot_left = jnp.concatenate([data_left[:edge_len], middle, south_left, north_left], 0)
        pot_right = jnp.concatenate([middle, data_right[:edge_len], south_right, north_right], 0)
        potentials[0][row_bit] = pot_left
        potentials[1][row_bit] = pot_right
        fluxes[0][row_bit] = product(blocks[0, row_bit], pot_left)
        fluxes[1][row_bit] = product(blocks[1, row_bit], pot_right)
    pot_all = jnp.stack([jnp.stack(potentials[0]), jnp.stack(potentials[1])])
    flux_all = jnp.stack([jnp.stack(fluxes[0]), jnp.stack(fluxes[1])])
    return (pot_all, flux_all)

def reference(leaf_maps, edge_data):
    full_len = leaf_maps.shape[-1]
    groups = BOX_COLS // 2 * (BOX_ROWS // 2)
    blocks = leaf_maps.reshape(2, BOX_COLS // 2, 2, BOX_ROWS // 2, full_len, full_len)
    blocks = blocks.transpose(1, 3, 0, 2, 4, 5).reshape(groups, 2, 2, full_len, full_len)
    data = edge_data.reshape(2, BOX_COLS // 2, 2, BOX_ROWS // 2, 2 * EDGE, RHS_COUNT)
    data = data.transpose(1, 3, 0, 2, 4, 5).reshape(groups, 2, 2, 2 * EDGE, RHS_COUNT)
    pot_all, flux_all = lax.map(group_solve, (blocks, data))

    def unfold(values):
        values = values.reshape(BOX_COLS // 2, BOX_ROWS // 2, 2, 2, full_len, RHS_COUNT)
        return values.transpose(2, 0, 3, 1, 4, 5).reshape(BOX_COLS, BOX_ROWS, full_len, RHS_COUNT)
    return (unfold(pot_all), unfold(flux_all))
```

```python
import functools

import jax
import jax.numpy as jnp
from jax import lax
from jax.experimental import pallas as pl
from jax.experimental.pallas import tpu as pltpu
from jax.sharding import PartitionSpec as P

HIGHEST = lax.Precision.HIGHEST
F32 = jnp.float32
BF16 = jnp.bfloat16
LANES = 128
PANEL = 8
TURN = 4


def exchange(block, axis):
    half = lax.axis_size(axis) // 2
    return lax.ppermute(block, axis, [(i, i ^ half) for i in range(2 * half)])


def side(axis):
    return (lax.axis_index(axis) >= lax.axis_size(axis) // 2).astype(jnp.int32)


def edges():
    c, r = side("gx"), side("gy")
    return 1 - c, c, 3 - r, 2 + r


def contract(left, right, dims):
    return lax.dot_general(left, right, ((dims[:1], dims[1:]), ((), ())), precision=HIGHEST, preferred_element_type=F32)


def full_nn(left, right):
    return contract(left, right, (1, 0))


def full_nt(left, right):
    return contract(left, right, (1, 1))


def full_tn(left, right):
    return contract(left, right, (0, 0))


def split(values):
    high = values.astype(BF16)
    return high, (values - high.astype(F32)).astype(BF16)


def half_dot(left, right):
    return jnp.dot(left, right, preferred_element_type=F32)


def triple(left, right):
    (lh, ll), (rh, rl) = left, right
    return half_dot(lh, rh) + (half_dot(lh, rl) + half_dot(ll, rh))


def tree(terms):
    while len(terms) > 1:
        terms = [a + b for a, b in zip(terms[::2], terms[1::2])]
    return terms[0]


def entry(i, j):
    return (i, j) if i >= j else (j, i)


def invert_panel(s):
    s = dict(s)
    for k in range(PANEL):
        inverse = 1.0 / s[k, k]
        rest = [i for i in range(PANEL) if i != k]
        column = {i: s[entry(i, k)] for i in rest}
        scaled = {i: column[i] * inverse for i in rest}
        for i in rest:
            for j in rest:
                if j <= i:
                    s[i, j] = s[i, j] - scaled[i] * column[j]
        for i in rest:
            s[entry(i, k)] = scaled[i]
        s[k, k] = -inverse
    return {key: -value for key, value in s.items()}


def invert_tile(tile):
    shape = (PANEL, LANES)
    lane = lax.broadcasted_iota(jnp.int32, shape, 1)
    sub = lax.broadcasted_iota(jnp.int32, shape, 0)
    count = LANES // PANEL

    def turn(_, rows):
        rows = list(rows)
        for q in range(TURN):
            start = PANEL * q
            panel = rows[q]
            columns = [jnp.broadcast_to(panel[:, start + j : start + j + 1], shape) for j in range(PANEL)]
            s = {(i, j): jnp.broadcast_to(columns[j][i : i + 1, :], shape) for i in range(PANEL) for j in range(i + 1)}
            inverse = invert_panel(s)
            inside = (lane >= start) & (lane < start + PANEL)
            unit = jnp.where(inside, jnp.where(lane - start == sub, 1.0, 0.0), panel)
            wide = [jnp.broadcast_to(unit[j : j + 1, :], shape) for j in range(PANEL)]
            swept = [tree([inverse[entry(i, j)] * wide[j] for j in range(PANEL)]) for i in range(PANEL)]
            new = swept[0]
            for i in range(1, PANEL):
                new = jnp.where(sub == i, swept[i], new)
            for p in [*range(q + 1, count), *range(q)]:
                row = rows[p]
                terms = [jnp.broadcast_to(row[:, start + j : start + j + 1], shape) * swept[j] for j in range(PANEL)]
                rows[p] = jnp.where(inside, 0.0, row) - tree(terms)
            rows[q] = new
        return tuple(pltpu.roll(row, LANES - PANEL * TURN, 1) for row in rows[TURN:] + rows[:TURN])

    rows = tuple(tile[PANEL * i : PANEL * (i + 1), :] for i in range(count))
    return jnp.concatenate(lax.fori_loop(0, count // TURN, turn, rows), 0)


def invert(matrix):
    size = matrix.shape[0]
    if size == LANES:
        return invert_tile(matrix)
    half = size // 2
    first, cross, last = matrix[:half, :half], matrix[:half, half:], matrix[half:, half:]
    head = invert(first)
    reach = full_nn(head, cross)
    tail = invert(last - full_tn(cross, reach))
    return join(head, reach, tail)


def join(head, reach, tail):
    corner = full_nn(reach, tail)
    top = jnp.concatenate([head + full_nt(corner, reach), -corner], 1)
    return jnp.concatenate([top, jnp.concatenate([-corner.T, tail], 1)], 0)


def unpack(packed):
    h = packed.shape[1] // 2
    low = jnp.concatenate([packed[h:, :h], packed[h:, h:]], 0)
    return jnp.concatenate(
        [jnp.concatenate([packed[:h, :h], low.T], 1), jnp.concatenate([low, packed[:h, h:]], 1)], 0
    )


def quarters(leaf, n, a, b):
    h = n // 2

    def block(row, rows, col):
        return leaf.at[pl.ds(pl.multiple_of(a * n + row, h // 2), rows), pl.ds(pl.multiple_of(b * n + col, h), h)]

    return block


def fetch(moves, sems):
    copies = [pltpu.make_async_copy(a, b, sems.at[k]) for k, (a, b) in enumerate(moves)]
    for copy in copies:
        copy.start()
    for copy in copies:
        copy.wait()


def symmetric(leaf, e, out, base):
    n = out.shape[1]
    h = n // 2
    block = quarters(leaf, n, e, e)
    return [
        (block(0, h, 0), out.at[pl.ds(base, h), pl.ds(0, h)]),
        (block(h, h, h), out.at[pl.ds(base, h), pl.ds(h, h)]),
        (block(h, h // 2, 0), out.at[pl.ds(base + h, h // 2), pl.ds(0, h)]),
        (block(h + h // 2, h // 2, 0), out.at[pl.ds(base + h, h // 2), pl.ds(h, h)]),
    ]


def joined_kernel(leaf, out, sems):
    fetch(symmetric(leaf, edges()[0], out, 0), sems)


def crossing_kernel(leaf, out, sems):
    n = out.shape[1]
    i, _, y, _ = edges()
    whole = leaf.at[pl.ds(pl.multiple_of(y * n, n), n), pl.ds(pl.multiple_of(i * n, n), n)]
    fetch([(whole, out.at[pl.ds(0, n)])] + symmetric(leaf, y, out, n), sems)


def passing_kernel(middle, middle_z, out):
    n = out.shape[1]
    out[:n] = middle[:n]
    out[n : 2 * n] = middle_z[:n]
    out[2 * n :] = middle[n:] + middle_z[n:]


def sum_kernel(own, other, out):
    out[...] = own[...] + other[...]


def outer_rows(leaf, edge, rows, sems):
    n = rows.shape[0]
    _, x, _, d = edges()
    own = pl.ds(pl.multiple_of(edge * n, n), n)
    return [
        pltpu.make_async_copy(leaf.at[own, pl.ds(pl.multiple_of(e * n, n), n)], rows.at[:, pl.ds(p * n, n)], sems.at[p])
        for p, e in enumerate((x, d))
    ]


def side_kernel(base, leaf, data, out, rows, held, sems):
    copies = outer_rows(leaf, edges()[0], rows, sems)
    copies.append(pltpu.make_async_copy(data.at[:, pl.ds(base, held.shape[1])], held, sems.at[2]))
    for copy in copies:
        copy.start()
    for copy in copies:
        copy.wait()
    out[...] = triple(split(rows[...]), split(held[...]))


def known_kernel(leaf, data, flux, high, low, potential, data_high, data_low, sems):
    step = pl.program_id(0)
    n = leaf.shape[0]
    i, x, y, d = edges()
    copies = [
        pltpu.make_async_copy(data.at[pl.ds(p * n, n), :], potential.at[pl.ds(pl.multiple_of(e * n, n), n), :], sems.at[p])
        for p, e in enumerate((x, d))
    ]

    @pl.when(step == 0)
    def _():
        for copy in copies:
            copy.start()
        data_high[...], data_low[...] = split(data[...])

    cols = lambda e: leaf[:, pl.ds(pl.multiple_of(e * n, n), n)]
    unknown = split(jnp.concatenate([cols(i), cols(y)], 1))
    high[...], low[...] = unknown
    outer = split(jnp.concatenate([cols(x), cols(d)], 1))
    flux[...] = triple(outer, (data_high[...], data_low[...]))

    @pl.when(step == pl.num_programs(0) - 1)
    def _():
        for copy in copies:
            copy.wait()


def first_kernel(joined, joined_far, middle, inverse, across, half):
    n = inverse.shape[0]
    h = n // 2
    solved = invert(unpack(joined[...] + joined_far[...]))
    inverse[...] = solved
    across[...] = full_nt(solved, middle[:n])

    def fill(diagonal, low):
        half[:h] = diagonal
        half[h:] = low

    @pl.when(side("gx") == 0)
    def _():
        fill(solved[:h, :h], solved[h : h + h // 2, :h])

    @pl.when(side("gx") == 1)
    def _():
        fill(solved[h:, h:], solved[h + h // 2 :, :h])


def middle_kernel(base, offset, widths, leaf, data, own, far, across, inverse, *rest):
    outs, (start, rows, held, sems) = rest[:-4], rest[-4:]
    width = sum(widths)
    copies = outer_rows(leaf, edges()[2], rows, sems)
    copies.append(pltpu.make_async_copy(data.at[:, pl.ds(base, width)], held, sems.at[2]))
    for copy in copies:
        copy.start()
    right = split(own[:, offset : offset + width] + far[:, offset : offset + width])
    start[...] = -triple(split(inverse[...]), right)
    out = triple(split(across[...].T), right)
    for copy in copies:
        copy.wait()
    out = triple(split(rows[...]), split(held[...])) - out
    done = 0
    for ref, part in zip(outs, widths):
        ref[...] = out[:, done : done + part]
        done += part


def build_kernel(middle, middle_z, passed, inverse, half_z, half_x, across, across_far, own, off, far, other):
    n = inverse.shape[0]
    h = n // 2

    def fill(one, two):
        low = jnp.concatenate([one[h:], two[h:]], 0)
        other[:h, :h] = one[:h]
        other[h:, h:] = two[:h]
        other[h:, :h] = low
        other[:h, h:] = low.T

    @pl.when(side("gx") == 0)
    def _():
        fill(half_z, half_x)

    @pl.when(side("gx") == 1)
    def _():
        fill(half_x, half_z)

    q_far = full_nt(inverse[...], passed[:n])
    across_far[...] = q_far
    q_own = across[...]
    p_own = full_nt(other[...], middle_z[:n])
    p_far = full_nt(other[...], passed[n : 2 * n])
    own[...] = unpack(middle[n:] + middle_z[n:]) - (full_nn(middle[:n], q_own) + full_nn(middle_z[:n], p_own))
    off[...] = -(full_nn(middle[:n], q_far) + full_nn(middle_z[:n], p_far))
    far[...] = unpack(passed[2 * n :]) - (full_nn(passed[:n], q_far) + full_nn(passed[n : 2 * n], p_far))


def open_half(matrix, head, reach, rest):
    h = matrix.shape[0] // 2
    solved = invert(matrix[:h, :h])
    head[...] = solved
    reach[...] = full_nn(solved, matrix[:h, h:])
    rest[...] = matrix[h:, h:] - full_tn(matrix[:h, h:], reach[...])


def head_kernel(matrix, head, reach, rest):
    open_half(matrix, head, reach, rest)


def turn_kernel(head, reach, rest, off, far, done, wide, left):
    done[...] = join(head[...], reach[...], invert(rest[...]))
    wide[...] = full_nn(done[...], off[...])
    left[...] = far[...] - full_tn(off[...], wide[...])


def tail_kernel(head, reach, rest, done, wide, out):
    out[...] = join(done[...], wide[...], join(head[...], reach[...], invert(rest[...])))


def beside(parts):
    return jnp.concatenate([part[...] for part in parts], 1)


def last_kernel(count, base, offset, inverse2, across, across_far, high, low, *rest):
    w_own, w_far, start = rest[:count], rest[count : 2 * count], rest[2 * count : 3 * count]
    _, _, flux, potential, solved, known, sems = rest[3 * count :]
    n = across.shape[0]
    width = solved.shape[1]
    i, _, y, _ = edges()
    cols = pl.ds(base, width)
    load = pltpu.make_async_copy(flux.at[:, cols], known, sems.at[2])
    load.start()
    top = triple(split(inverse2[...]), split(jnp.concatenate([beside(w_own), beside(w_far)], 0)))
    left = split(jnp.concatenate([across[...], across_far[...]], 1))
    solved[:n] = beside(start)[:, offset : offset + width] + triple(left, split(top))
    solved[n:] = -top[:n]
    copies = [
        pltpu.make_async_copy(
            solved.at[pl.ds(p * n, n), :], potential.at[pl.ds(pl.multiple_of(e * n, n), n), cols], sems.at[p]
        )
        for p, e in enumerate((i, y))
    ]
    for copy in copies:
        copy.start()
    load.wait()
    known[...] += triple((high[...], low[...]), split(solved[...]))
    store = pltpu.make_async_copy(known, flux.at[:, cols], sems.at[2])
    store.start()
    for copy in copies + [store]:
        copy.wait()


def array(*shape, dtype=F32):
    return jax.ShapeDtypeStruct(shape, dtype)


ANY = pl.BlockSpec(memory_space=pl.ANY)
HBM = pl.BlockSpec(memory_space=pltpu.HBM)
WHOLE = pl.BlockSpec(memory_space=pltpu.VMEM)
MIB = 1 << 20


COSTS = {
    "crossing": 0.1,
    "joined": 0.1,
    "side": 1.0,
    "first": 11.0,
    "middle": 1.3,
    "passing": 0.1,
    "known": 6.0,
    "build": 3.0,
    "head": 5.4,
    "turn": 6.5,
    "tail": 6.6,
    "total": 0.1,
    "last": 5.0,
}


class Chain:
    def __init__(self):
        self.mark = None

    def __call__(self, name, kernel, outs, *args, ins=None, out_specs=None, scratch=(), aliases=None, limit=24, **kwargs):
        cost = COSTS[name]
        ins = ins or [WHOLE] * len(args)
        out_specs = out_specs or [WHOLE] * len(outs)
        marks = [] if self.mark is None else [self.mark]

        def body(*refs):
            inner = refs[: len(args)] + refs[len(args) + len(marks) :]
            kernel(*inner[: len(args) + len(outs)], *inner[len(args) + len(outs) + 1 :])

        *given, self.mark = pl.pallas_call(
            body,
            out_shape=list(outs) + [array(8, LANES)],
            in_specs=list(ins) + [HBM] * len(marks),
            out_specs=list(out_specs) + [HBM],
            scratch_shapes=list(scratch),
            input_output_aliases=aliases or {},
            compiler_params=pltpu.CompilerParams(vmem_limit_bytes=limit * MIB),
            cost_estimate=pl.CostEstimate(flops=int(cost * 1e9), bytes_accessed=int(cost * 3e6), transcendentals=0),
            name=name,
            **kwargs,
        )(*args, *marks)
        return given[0] if len(given) == 1 else given


def per_device(leaf_maps, edge_data):
    leaf = leaf_maps[0, 0]
    data = edge_data[0, 0]
    full, count = leaf.shape[0], data.shape[1]
    n = full // 4
    h = n // 2
    packed = 3 * n // 4
    dma = pltpu.SemaphoreType.DMA
    call = Chain()
    unit = count // 8
    widths = [2 * unit, 3 * unit, 2 * unit, unit]
    bases = [0, 2 * unit, 5 * unit, 7 * unit]
    cut = 5 * unit

    middle = call("crossing", crossing_kernel, [array(n + packed, n)], leaf, ins=[ANY], scratch=[dma((5,))])
    middle_z = exchange(middle, "gy")
    joined = call("joined", joined_kernel, [array(packed, n)], leaf, ins=[ANY], scratch=[dma((4,))])
    joined_far = exchange(joined, "gx")

    def sides(base, width):
        own = call(
            "side",
            functools.partial(side_kernel, base),
            [array(n, width)],
            leaf,
            data,
            ins=[ANY] * 2,
            scratch=[pltpu.VMEM((n, 2 * n), F32), pltpu.VMEM((2 * n, width), F32), dma((3,))],
        )
        return own, exchange(own, "gx")

    def middles(parts, offset, own, far):
        base, width = bases[parts[0]], sum(widths[k] for k in parts)
        given = call(
            "middle",
            functools.partial(middle_kernel, base, base - offset, [widths[k] for k in parts]),
            [array(n, widths[k]) for k in parts] + [array(n, width)],
            leaf,
            data,
            own,
            far,
            across,
            inverse1,
            ins=[ANY] * 2 + [WHOLE] * 4,
            scratch=[pltpu.VMEM((n, 2 * n), F32), pltpu.VMEM((2 * n, width), F32), dma((3,))],
        )
        return given[:-1], given[-1]

    def total(own, other):
        return call("total", sum_kernel, [array(*own.shape)], own, other)

    own_a, far_a = sides(0, cut)
    inverse1, across, half = call(
        "first", first_kernel, [array(n, n)] * 2 + [array(packed, h)], joined, joined_far, middle
    )
    half_z = exchange(half, "gy")
    (v0,), start0 = middles([0], 0, own_a, far_a)
    z0 = exchange(v0, "gy")
    passing = call("passing", passing_kernel, [array(2 * n + packed, n)], middle, middle_z)
    passed = exchange(passing, "gx")
    known, high, low, potential = call(
        "known",
        known_kernel,
        [
            array(full, count),
            array(full, 2 * n, dtype=BF16),
            array(full, 2 * n, dtype=BF16),
            array(full, count),
        ],
        leaf,
        data,
        ins=[pl.BlockSpec((n, full), lambda s: (s, 0)), pl.BlockSpec((2 * n, count), lambda s: (0, 0))],
        out_specs=[
            pl.BlockSpec((n, count), lambda s: (s, 0)),
            pl.BlockSpec((n, 2 * n), lambda s: (s, 0)),
            pl.BlockSpec((n, 2 * n), lambda s: (s, 0)),
            ANY,
        ],
        scratch=[pltpu.VMEM((2 * n, count), BF16), pltpu.VMEM((2 * n, count), BF16), dma((2,))],
        grid=(4,),
    )
    half_x = exchange(half_z, "gx")
    (v1,), start1 = middles([1], 0, own_a, far_a)
    z1 = exchange(v1, "gy")
    own_b, far_b = sides(cut, count - cut)
    across_far, s_own, s_off, s_far = call(
        "build",
        build_kernel,
        [array(n, n)] * 4,
        middle,
        middle_z,
        passed,
        inverse1,
        half_z,
        half_x,
        across,
        scratch=[pltpu.VMEM((n, n), F32)],
    )
    head, reach, rest = call("head", head_kernel, [array(h, h)] * 3, s_own)
    w0 = total(v0, z0)
    w0_far = exchange(w0, "gx")
    (v2, v3), start2 = middles([2, 3], cut, own_b, far_b)
    z2, z3 = exchange(v2, "gy"), exchange(v3, "gy")
    done, wide, left = call("turn", turn_kernel, [array(n, n)] * 3, head, reach, rest, s_off, s_far)
    w1 = total(v1, z1)
    w1_far = exchange(w1, "gx")
    head, reach, rest = call("head", head_kernel, [array(h, h)] * 3, left)
    inverse2 = call("tail", tail_kernel, [array(2 * n, 2 * n)], head, reach, rest, done, wide)
    w2 = total(v2, z2)
    w2_far = exchange(w2, "gx")
    w3 = total(v3, z3)
    w3_far = exchange(w3, "gx")

    flux = known
    groups = [
        ([0, 1], [w0, w1], [w0_far, w1_far], [start0, start1]),
        ([2], [w2], [w2_far], [start2]),
        ([3], [w3], [w3_far], [start2]),
    ]
    for parts, own, far, start in groups:
        base, width = bases[parts[0]], sum(widths[k] for k in parts)
        pieces = (*own, *far, *start)
        offset = widths[2] if parts == [3] else 0
        flux, potential = call(
            "last",
            functools.partial(last_kernel, len(parts), base, offset),
            [array(full, count), array(full, count)],
            inverse2,
            across,
            across_far,
            high,
            low,
            *pieces,
            flux,
            potential,
            ins=[WHOLE] * (5 + len(pieces)) + [ANY] * 2,
            out_specs=[ANY] * 2,
            scratch=[pltpu.VMEM((2 * n, width), F32), pltpu.VMEM((full, width), F32), dma((3,))],
            aliases={5 + len(pieces): 0, 6 + len(pieces): 1},
        )
    return potential[None, None], flux[None, None]


def solution(mesh):
    spec = P("gx", "gy", None, None)
    return jax.shard_map(per_device, mesh=mesh, in_specs=(spec, spec), out_specs=(spec, spec), check_vma=False)
```

```python
import functools

import jax
import jax.numpy as jnp
from jax import lax
from jax.experimental import pallas as pl
from jax.experimental.pallas import tpu as pltpu
from jax.sharding import PartitionSpec as P

HIGHEST = lax.Precision.HIGHEST
F32 = jnp.float32
BF16 = jnp.bfloat16
LANES = 128
PANEL = 8
TURN = 8


def exchange(block, axis):
    half = lax.axis_size(axis) // 2
    return lax.ppermute(block, axis, [(i, i ^ half) for i in range(2 * half)])


def side(axis):
    return (lax.axis_index(axis) >= lax.axis_size(axis) // 2).astype(jnp.int32)


def edges():
    c, r = side("gx"), side("gy")
    return 1 - c, c, 3 - r, 2 + r


def contract(left, right, dims):
    return lax.dot_general(left, right, ((dims[:1], dims[1:]), ((), ())), precision=HIGHEST, preferred_element_type=F32)


def full_nn(left, right):
    return contract(left, right, (1, 0))


def full_nt(left, right):
    return contract(left, right, (1, 1))


def full_tn(left, right):
    return contract(left, right, (0, 0))


def split(values):
    high = values.astype(BF16)
    return high, (values - high.astype(F32)).astype(BF16)


def half_dot(left, right):
    return jnp.dot(left, right, preferred_element_type=F32)


def triple(left, right):
    (lh, ll), (rh, rl) = left, right
    return half_dot(lh, rh) + (half_dot(lh, rl) + half_dot(ll, rh))


def near_nn(left, right):
    return triple(split(left), split(right))


def near_nt(left, right):
    return near_nn(left, right.T)


def near_tn(left, right):
    return near_nn(left.T, right)


def tree(terms):
    while len(terms) > 1:
        terms = [a + b for a, b in zip(terms[::2], terms[1::2])]
    return terms[0]


def entry(i, j):
    return (i, j) if i >= j else (j, i)


def invert_panel(s):
    s = dict(s)
    for k in range(PANEL):
        inverse = 1.0 / s[k, k]
        rest = [i for i in range(PANEL) if i != k]
        column = {i: s[entry(i, k)] for i in rest}
        scaled = {i: column[i] * inverse for i in rest}
        for i in rest:
            for j in rest:
                if j <= i:
                    s[i, j] = s[i, j] - scaled[i] * column[j]
        for i in rest:
            s[entry(i, k)] = scaled[i]
        s[k, k] = -inverse
    return {key: -value for key, value in s.items()}


def invert_tile(tile):
    shape = (PANEL, LANES)
    lane = lax.broadcasted_iota(jnp.int32, shape, 1)
    sub = lax.broadcasted_iota(jnp.int32, shape, 0)
    count = LANES // PANEL

    def turn(_, rows):
        rows = list(rows)
        for q in range(TURN):
            start = PANEL * q
            panel = rows[q]
            columns = [jnp.broadcast_to(panel[:, start + j : start + j + 1], shape) for j in range(PANEL)]
            s = {(i, j): jnp.broadcast_to(columns[j][i : i + 1, :], shape) for i in range(PANEL) for j in range(i + 1)}
            inverse = invert_panel(s)
            inside = (lane >= start) & (lane < start + PANEL)
            unit = jnp.where(inside, jnp.where(lane - start == sub, 1.0, 0.0), panel)
            wide = [jnp.broadcast_to(unit[j : j + 1, :], shape) for j in range(PANEL)]
            swept = [tree([inverse[entry(i, j)] * wide[j] for j in range(PANEL)]) for i in range(PANEL)]
            new = swept[0]
            for i in range(1, PANEL):
                new = jnp.where(sub == i, swept[i], new)
            for p in [*range(q + 1, count), *range(q)]:
                row = rows[p]
                terms = [jnp.broadcast_to(row[:, start + j : start + j + 1], shape) * swept[j] for j in range(PANEL)]
                rows[p] = jnp.where(inside, 0.0, row) - tree(terms)
            rows[q] = new
        return tuple(pltpu.roll(row, LANES - PANEL * TURN, 1) for row in rows[TURN:] + rows[:TURN])

    rows = tuple(tile[PANEL * i : PANEL * (i + 1), :] for i in range(count))
    return jnp.concatenate(lax.fori_loop(0, count // TURN, turn, rows), 0)


def invert(matrix):
    size = matrix.shape[0]
    if size == LANES:
        return invert_tile(matrix)
    half = size // 2
    first, cross, last = matrix[:half, :half], matrix[:half, half:], matrix[half:, half:]
    head = invert(first)
    reach = full_nn(head, cross)
    tail = invert(last - full_tn(cross, reach))
    return join(head, reach, tail)


def join(head, reach, tail):
    corner = full_nn(reach, tail)
    top = jnp.concatenate([head + full_nt(corner, reach), -corner], 1)
    return jnp.concatenate([top, jnp.concatenate([-corner.T, tail], 1)], 0)


def near_join(head, reach, tail):
    corner = near_nn(reach, tail)
    top = jnp.concatenate([head + near_nt(corner, reach), -corner], 1)
    return jnp.concatenate([top, jnp.concatenate([-corner.T, tail], 1)], 0)


def unpack(packed):
    h = packed.shape[1] // 2
    low = jnp.concatenate([packed[h:, :h], packed[h:, h:]], 0)
    return jnp.concatenate(
        [jnp.concatenate([packed[:h, :h], low.T], 1), jnp.concatenate([low, packed[:h, h:]], 1)], 0
    )


def quarters(leaf, n, a, b):
    h = n // 2

    def block(row, rows, col):
        return leaf.at[pl.ds(pl.multiple_of(a * n + row, h // 2), rows), pl.ds(pl.multiple_of(b * n + col, h), h)]

    return block


def fetch(moves, sems):
    copies = [pltpu.make_async_copy(a, b, sems.at[k]) for k, (a, b) in enumerate(moves)]
    for copy in copies:
        copy.start()
    for copy in copies:
        copy.wait()


def symmetric(leaf, e, out, base):
    n = out.shape[1]
    h = n // 2
    block = quarters(leaf, n, e, e)
    return [
        (block(0, h, 0), out.at[pl.ds(base, h), pl.ds(0, h)]),
        (block(h, h, h), out.at[pl.ds(base, h), pl.ds(h, h)]),
        (block(h, h // 2, 0), out.at[pl.ds(base + h, h // 2), pl.ds(0, h)]),
        (block(h + h // 2, h // 2, 0), out.at[pl.ds(base + h, h // 2), pl.ds(h, h)]),
    ]


def passing_kernel(middle, middle_z, out):
    n = out.shape[1]
    out[:n] = middle_z[:n]
    out[n:] = middle[n:] + middle_z[n:]


def relay_kernel(given, out):
    out[...] = given[...]


def sum_kernel(own, other, out):
    out[...] = own[...] + other[...]


def append_kernel(before, own, other, out):
    width = before.shape[1]
    out[:, :width] = before[...]
    out[:, width:] = own[...] + other[...]


def outer_rows(leaf, edge, rows, sems):
    n = rows.shape[0]
    _, x, _, d = edges()
    own = pl.ds(pl.multiple_of(edge * n, n), n)
    return [
        pltpu.make_async_copy(leaf.at[own, pl.ds(pl.multiple_of(e * n, n), n)], rows.at[:, pl.ds(p * n, n)], sems.at[p])
        for p, e in enumerate((x, d))
    ]


def side_kernel(base, leaf, data, out, rows, held, sems):
    n, width = rows.shape[0], held.shape[1]
    i, _, y, _ = edges()
    copies = outer_rows(leaf, i, rows, sems)
    copies.append(pltpu.make_async_copy(data.at[:, pl.ds(base, width)], held, sems.at[2]))
    for copy in copies:
        copy.start()
    if out.shape[1] > width:
        whole = leaf.at[pl.ds(pl.multiple_of(y * n, n), n), pl.ds(pl.multiple_of(i * n, n), n)]
        fetch([(whole, out.at[:, pl.ds(width, n)])], sems.at[pl.ds(3, 1)])
    for copy in copies:
        copy.wait()
    out[:, :width] = triple(split(rows[...]), split(held[...]))


def joined_kernel(leaf, out, sems):
    fetch(symmetric(leaf, edges()[0], out, 0), sems)


def crossing_kernel(leaf, out, sems):
    n = out.shape[1]
    i, _, y, _ = edges()
    whole = leaf.at[pl.ds(pl.multiple_of(y * n, n), n), pl.ds(pl.multiple_of(i * n, n), n)]
    fetch([(whole, out.at[pl.ds(0, n)])] + symmetric(leaf, y, out, n), sems)


def known_kernel(leaf, data, flux, high, low, potential, _, data_high, data_low, sems):
    step = pl.program_id(0)
    n = leaf.shape[0]
    i, x, y, d = edges()
    copies = [
        pltpu.make_async_copy(data.at[pl.ds(p * n, n), :], potential.at[pl.ds(pl.multiple_of(e * n, n), n), :], sems.at[p])
        for p, e in enumerate((x, d))
    ]

    @pl.when(step == 0)
    def _():
        for copy in copies:
            copy.start()
        data_high[...], data_low[...] = split(data[...])

    cols = lambda e: leaf[:, pl.ds(pl.multiple_of(e * n, n), n)]
    unknown = split(jnp.concatenate([cols(i), cols(y)], 1))
    high[...], low[...] = unknown
    outer = split(jnp.concatenate([cols(x), cols(d)], 1))
    flux[...] = triple(outer, (data_high[...], data_low[...]))

    @pl.when(step == pl.num_programs(0) - 1)
    def _():
        for copy in copies:
            copy.wait()


def first_kernel(joined, joined_far, middle, inverse, across, half):
    n = inverse.shape[0]
    h = n // 2
    solved = invert(unpack(joined[...] + joined_far[...]))
    inverse[...] = solved
    across[...] = near_nt(solved, middle[:n])

    def fill(diagonal, low):
        half[:h] = diagonal
        half[h:] = low

    @pl.when(side("gx") == 0)
    def _():
        fill(solved[:h, :h], solved[h : h + h // 2, :h])

    @pl.when(side("gx") == 1)
    def _():
        fill(solved[h:, h:], solved[h + h // 2 :, :h])


def middle_kernel(base, offset, widths, leaf, data, own, far, across, inverse, *rest):
    outs, (start, rows, held, sems) = rest[:-4], rest[-4:]
    width = sum(widths)
    copies = outer_rows(leaf, edges()[2], rows, sems)
    copies.append(pltpu.make_async_copy(data.at[:, pl.ds(base, width)], held, sems.at[2]))
    for copy in copies:
        copy.start()
    right = split(own[:, offset : offset + width] + far[:, offset : offset + width])
    start[...] = -triple(split(inverse[...]), right)
    out = triple(split(across[...].T), right)
    for copy in copies:
        copy.wait()
    out = triple(split(rows[...]), split(held[...])) - out
    done = 0
    for ref, part in zip(outs, widths):
        ref[...] = out[:, done : done + part]
        done += part


def build_kernel(middle, middle_z, passed, side_far, inverse, half_z, half_x, across, across_far, own, off, far, other):
    n = inverse.shape[0]
    h = n // 2

    def fill(one, two):
        low = jnp.concatenate([one[h:], two[h:]], 0)
        other[:h, :h] = one[:h]
        other[h:, h:] = two[:h]
        other[h:, :h] = low
        other[:h, h:] = low.T

    @pl.when(side("gx") == 0)
    def _():
        fill(half_z, half_x)

    @pl.when(side("gx") == 1)
    def _():
        fill(half_x, half_z)

    cross = side_far[:, -n:]
    q_far = near_nt(inverse[...], cross)
    q_own = across[...]
    across_far[...] = q_far
    p_own = near_nt(other[...], middle_z[:n])
    p_far = near_nt(other[...], passed[:n])
    own[...] = unpack(middle[n:] + middle_z[n:]) - (near_nn(middle[:n], q_own) + near_nn(middle_z[:n], p_own))
    off[...] = -(near_nn(middle[:n], q_far) + near_nn(middle_z[:n], p_far))
    far[...] = unpack(passed[n:]) - (near_nn(cross, q_far) + near_nn(passed[:n], p_far))


def open_half(matrix, head, reach, rest):
    h = matrix.shape[0] // 2
    solved = invert(matrix[:h, :h])
    head[...] = solved
    reach[...] = full_nn(solved, matrix[:h, h:])
    rest[...] = matrix[h:, h:] - full_tn(matrix[:h, h:], reach[...])


def head_kernel(matrix, head, reach, rest):
    open_half(matrix, head, reach, rest)


def turn_kernel(head, reach, rest, off, far, done, wide, left):
    done[...] = join(head[...], reach[...], invert(rest[...]))
    wide[...] = near_nn(done[...], off[...])
    left[...] = far[...] - near_tn(off[...], wide[...])


def tail_kernel(head, reach, rest, done, wide, across, across_far, high, low):
    n = done.shape[0]
    solved = near_join(done[...], wide[...], join(head[...], reach[...], invert(rest[...])))
    inward = triple(split(jnp.concatenate([across[...], across_far[...]], 1)), split(solved))
    high[...], low[...] = split(jnp.concatenate([inward, -solved[:n]], 0))


def last_kernel(count, base, solve_high, solve_low, high, low, known, *rest):
    w_own, w_far, starts = rest[:count], rest[count : 2 * count], rest[2 * count : -7]
    flux, potential, solved, made, sems = rest[-5:]
    n, width = w_own[0].shape[0], solved.shape[1]
    i, _, y, _ = edges()
    cols = pl.ds(base, width)
    done = 0
    for own, far in zip(w_own, w_far):
        part = slice(done, done + own.shape[1])
        inner = triple((solve_high[...], solve_low[...]), split(jnp.concatenate([own[...], far[...]], 0)))
        solved[:, part] = inner
        done = part.stop
    done = 0
    for start in starts:
        part = slice(done, done + start.shape[1])
        solved[:n, part] += start[...]
        done = part.stop
    right = split(solved[...])
    copies = []
    for k in range(4):
        rows = pl.ds(k * n, n)
        made[rows] = known[rows, base : base + width] + triple((high[rows], low[rows]), right)
        copies.append(pltpu.make_async_copy(made.at[rows], flux.at[rows, cols], sems.at[k]))
        copies[-1].start()
    for p, e in enumerate((i, y)):
        rows = pl.ds(pl.multiple_of(e * n, n), n)
        copies.append(pltpu.make_async_copy(solved.at[pl.ds(p * n, n), :], potential.at[rows, cols], sems.at[4 + p]))
        copies[-1].start()
    for copy in copies:
        copy.wait()


def array(*shape, dtype=F32):
    return jax.ShapeDtypeStruct(shape, dtype)


ANY = pl.BlockSpec(memory_space=pl.ANY)
HBM = pl.BlockSpec(memory_space=pltpu.HBM)
WHOLE = pl.BlockSpec(memory_space=pltpu.VMEM)
MIB = 1 << 20
EARLY = 58


COSTS = {
    "passing": 8.0,
    "relay": 8.0,
    "build": 0.7,
    "opening": 1.2,
    "copy": 0.05,
    "closing": 2.0,
}


class Chain:
    def __init__(self):
        self.mark = None

    def __call__(self, name, kernel, outs, *args, ins=None, out_specs=None, scratch=(), aliases=None, limit=24, **kwargs):
        cost = COSTS.get(name, 0.005)
        ins = ins or [WHOLE] * len(args)
        out_specs = out_specs or [WHOLE] * len(outs)
        marks = [] if self.mark is None else [self.mark]

        def body(*refs):
            inner = refs[: len(args)] + refs[len(args) + len(marks) :]
            kernel(*inner[: len(args) + len(outs)], *inner[len(args) + len(outs) + 1 :])

        *given, self.mark = pl.pallas_call(
            body,
            out_shape=list(outs) + [array(8, LANES)],
            in_specs=list(ins) + [HBM] * len(marks),
            out_specs=list(out_specs) + [HBM],
            scratch_shapes=list(scratch),
            input_output_aliases=aliases or {},
            compiler_params=pltpu.CompilerParams(vmem_limit_bytes=limit * MIB),
            cost_estimate=pl.CostEstimate(flops=int(cost * 1e9), bytes_accessed=int(cost * 3e6), transcendentals=0),
            name=name,
            **kwargs,
        )(*args, *marks)
        return given[0] if len(given) == 1 else given


def per_device(leaf_maps, edge_data):
    leaf = leaf_maps[0, 0]
    data = edge_data[0, 0]
    full, count = leaf.shape[0], data.shape[1]
    n = full // 4
    h = n // 2
    packed = 3 * n // 4
    dma = pltpu.SemaphoreType.DMA
    call = Chain()
    unit = count // 8
    widths = [2 * unit, 2 * unit, 2 * unit, unit, unit]
    bases = [0, 2 * unit, 4 * unit, 6 * unit, 7 * unit]

    middle = call(
        "crossing", crossing_kernel, [array(n + packed, n)], leaf, limit=EARLY, ins=[HBM], scratch=[dma((5,))]
    )
    middle_z = exchange(middle, "gy")
    joined = call("joined", joined_kernel, [array(packed, n)], leaf, limit=EARLY, ins=[HBM], scratch=[dma((4,))])
    joined_far = exchange(joined, "gx")

    def sides(base, width, extra=0, limit=24):
        own = call(
            "side",
            functools.partial(side_kernel, base),
            [array(n, width + extra)],
            leaf,
            data,
            limit=limit,
            ins=[HBM] * 2,
            scratch=[pltpu.VMEM((n, 2 * n), F32), pltpu.VMEM((2 * n, width), F32), dma((4,))],
        )
        return own, exchange(own, "gx")

    def middles(parts, offset, own, far):
        base, width = bases[parts[0]], sum(widths[k] for k in parts)
        given = call(
            "middle",
            functools.partial(middle_kernel, base, base - offset, [widths[k] for k in parts]),
            [array(n, widths[k]) for k in parts] + [array(n, width)],
            leaf,
            data,
            own,
            far,
            across,
            inverse1,
            ins=[ANY] * 2 + [WHOLE] * 4,
            scratch=[pltpu.VMEM((n, 2 * n), F32), pltpu.VMEM((2 * n, width), F32), dma((3,))],
        )
        return given[:-1], given[-1]

    def total(own, far, name="total"):
        w = call(name, sum_kernel, [array(*own.shape)], own, far)
        return w, exchange(w, "gx")

    def copy(given, name="copy"):
        return call(name, relay_kernel, [array(*given.shape)], given)

    own_a, far_a = sides(0, 4 * unit, n, EARLY)
    inverse1, across, half = call(
        "first", first_kernel, [array(n, n)] * 2 + [array(packed, h)], joined, joined_far, middle
    )
    half_z = exchange(half, "gy")
    passing = call("passing", passing_kernel, [array(n + packed, n)], middle, middle_z)
    passed = exchange(passing, "gx")
    (v0,), start0 = middles([0], 0, own_a, far_a)
    z0 = exchange(v0, "gy")
    half_z = copy(half_z, "relay")
    half_x = exchange(half_z, "gx")
    (v1,), start1 = middles([1], 0, own_a, far_a)
    z1 = exchange(v1, "gy")
    own_b, far_b = sides(bases[2], widths[2])
    own_c, far_c = sides(bases[3], 2 * unit)
    known, high, low, potential, flux = call(
        "known",
        known_kernel,
        [
            array(full, count),
            array(full, 2 * n, dtype=BF16),
            array(full, 2 * n, dtype=BF16),
            array(full, count),
            array(full, count),
        ],
        leaf,
        data,
        ins=[pl.BlockSpec((n, full), lambda s: (s, 0)), pl.BlockSpec((2 * n, count), lambda s: (0, 0))],
        out_specs=[
            pl.BlockSpec((n, count), lambda s: (s, 0)),
            pl.BlockSpec((n, 2 * n), lambda s: (s, 0)),
            pl.BlockSpec((n, 2 * n), lambda s: (s, 0)),
            ANY,
            ANY,
        ],
        scratch=[pltpu.VMEM((2 * n, count), BF16), pltpu.VMEM((2 * n, count), BF16), dma((2,))],
        grid=(4,),
    )
    across_far, s_own, s_off, s_far = call(
        "build",
        build_kernel,
        [array(n, n)] * 4,
        middle,
        middle_z,
        passed,
        far_a,
        inverse1,
        half_z,
        half_x,
        across,
        scratch=[pltpu.VMEM((n, n), F32)],
    )
    head, reach, rest = call("head", head_kernel, [array(h, h)] * 3, s_own)
    w0 = call("opening", sum_kernel, [array(*v0.shape)], v0, z0)
    (v2,), start2 = middles([2], bases[2], own_b, far_b)
    z2 = exchange(v2, "gy")
    done, wide, left = call("turn", turn_kernel, [array(n, n)] * 3, head, reach, rest, s_off, s_far)
    w1 = call("append", append_kernel, [array(n, 4 * unit)], w0, v1, z1)
    w1_far = exchange(w1, "gx")
    (v3, v4), start3 = middles([3, 4], bases[3], own_c, far_c)
    z3 = exchange(v3, "gy")
    head, reach, rest = call("head", head_kernel, [array(h, h)] * 3, left)
    w2, w2_far = total(v2, z2)
    v4 = copy(v4)
    z4 = exchange(v4, "gy")
    inverse2 = call(
        "tail", tail_kernel, [array(2 * n, 2 * n, dtype=BF16)] * 2, head, reach, rest, done, wide, across, across_far
    )
    w3, w3_far = total(v3, z3)
    w4, w4_far = total(v4, z4, "closing")

    def last(base, own, far, starts, held):
        width = sum(part.shape[1] for part in own)
        fixed = 5 + 2 * len(own) + len(starts)
        return call(
            "last",
            functools.partial(last_kernel, len(own), base),
            [array(full, count), array(full, count)],
            *inverse2,
            high,
            low,
            known,
            *own,
            *far,
            *starts,
            *held[1:],
            *held[:1],
            ins=[WHOLE] * fixed + [ANY] * len(held),
            out_specs=[ANY] * 2,
            scratch=[pltpu.VMEM((2 * n, width), F32), pltpu.VMEM((full, width), F32), dma((6,))],
            aliases={fixed: 1, fixed + 1: 0},
        )

    held = last(0, [w1], [w1_far], [start0, start1], [flux, potential])
    held = last(bases[2], [w2], [w2_far], [start2], held)
    w3_far = copy(w3_far)
    held = last(bases[3], [w3, w4], [w3_far, w4_far], [start3], held)
    return held[1][None, None], held[0][None, None]


def solution(mesh):
    spec = P("gx", "gy", None, None)
    return jax.shard_map(per_device, mesh=mesh, in_specs=(spec, spec), out_specs=(spec, spec), check_vma=False)
```

```python
import functools

import jax
import jax.numpy as jnp
from jax import lax
from jax.experimental import pallas as pl
from jax.experimental.pallas import tpu as pltpu
from jax.sharding import PartitionSpec as P

HIGHEST = lax.Precision.HIGHEST
F32 = jnp.float32
BF16 = jnp.bfloat16
LANES = 128
PANEL = 8
TURN = 8


def exchange(block, axis):
    half = lax.axis_size(axis) // 2
    return lax.ppermute(block, axis, [(i, i ^ half) for i in range(2 * half)])


def side(axis):
    return (lax.axis_index(axis) >= lax.axis_size(axis) // 2).astype(jnp.int32)


def edges():
    c, r = side("gx"), side("gy")
    return 1 - c, c, 3 - r, 2 + r


def contract(left, right, dims):
    return lax.dot_general(left, right, ((dims[:1], dims[1:]), ((), ())), precision=HIGHEST, preferred_element_type=F32)


def full_nn(left, right):
    return contract(left, right, (1, 0))


def full_nt(left, right):
    return contract(left, right, (1, 1))


def full_tn(left, right):
    return contract(left, right, (0, 0))


def split(values):
    high = values.astype(BF16)
    return high, (values - high.astype(F32)).astype(BF16)


def half_dot(left, right):
    return jnp.dot(left, right, preferred_element_type=F32)


def triple(left, right):
    (lh, ll), (rh, rl) = left, right
    return half_dot(lh, rh) + (half_dot(lh, rl) + half_dot(ll, rh))


def near_nn(left, right):
    return triple(split(left), split(right))


def near_nt(left, right):
    return near_nn(left, right.T)


def near_tn(left, right):
    return near_nn(left.T, right)


def tree(terms):
    while len(terms) > 1:
        terms = [a + b for a, b in zip(terms[::2], terms[1::2])]
    return terms[0]


def entry(i, j):
    return (i, j) if i >= j else (j, i)


def invert_panel(s):
    s = dict(s)
    for k in range(PANEL):
        inverse = 1.0 / s[k, k]
        rest = [i for i in range(PANEL) if i != k]
        column = {i: s[entry(i, k)] for i in rest}
        scaled = {i: column[i] * inverse for i in rest}
        for i in rest:
            for j in rest:
                if j <= i:
                    s[i, j] = s[i, j] - scaled[i] * column[j]
        for i in rest:
            s[entry(i, k)] = scaled[i]
        s[k, k] = -inverse
    return {key: -value for key, value in s.items()}


def invert_tile(tile):
    shape = (PANEL, LANES)
    lane = lax.broadcasted_iota(jnp.int32, shape, 1)
    sub = lax.broadcasted_iota(jnp.int32, shape, 0)
    count = LANES // PANEL

    def turn(_, rows):
        rows = list(rows)
        for q in range(TURN):
            start = PANEL * q
            panel = rows[q]
            columns = [jnp.broadcast_to(panel[:, start + j : start + j + 1], shape) for j in range(PANEL)]
            s = {(i, j): jnp.broadcast_to(columns[j][i : i + 1, :], shape) for i in range(PANEL) for j in range(i + 1)}
            inverse = invert_panel(s)
            inside = (lane >= start) & (lane < start + PANEL)
            unit = jnp.where(inside, jnp.where(lane - start == sub, 1.0, 0.0), panel)
            wide = [jnp.broadcast_to(unit[j : j + 1, :], shape) for j in range(PANEL)]
            swept = [tree([inverse[entry(i, j)] * wide[j] for j in range(PANEL)]) for i in range(PANEL)]
            new = swept[0]
            for i in range(1, PANEL):
                new = jnp.where(sub == i, swept[i], new)
            for p in [*range(q + 1, count), *range(q)]:
                row = rows[p]
                terms = [jnp.broadcast_to(row[:, start + j : start + j + 1], shape) * swept[j] for j in range(PANEL)]
                rows[p] = jnp.where(inside, 0.0, row) - tree(terms)
            rows[q] = new
        return tuple(pltpu.roll(row, LANES - PANEL * TURN, 1) for row in rows[TURN:] + rows[:TURN])

    rows = tuple(tile[PANEL * i : PANEL * (i + 1), :] for i in range(count))
    return jnp.concatenate(lax.fori_loop(0, count // TURN, turn, rows), 0)


def invert(matrix):
    size = matrix.shape[0]
    if size == LANES:
        return invert_tile(matrix)
    half = size // 2
    first, cross, last = matrix[:half, :half], matrix[:half, half:], matrix[half:, half:]
    head = invert(first)
    reach = full_nn(head, cross)
    tail = invert(last - full_tn(cross, reach))
    return join(head, reach, tail)


def join(head, reach, tail):
    corner = full_nn(reach, tail)
    top = jnp.concatenate([head + full_nt(corner, reach), -corner], 1)
    return jnp.concatenate([top, jnp.concatenate([-corner.T, tail], 1)], 0)


def near_join(head, reach, tail):
    corner = near_nn(reach, tail)
    top = jnp.concatenate([head + near_nt(corner, reach), -corner], 1)
    return jnp.concatenate([top, jnp.concatenate([-corner.T, tail], 1)], 0)


def unpack(packed):
    h = packed.shape[1] // 2
    low = jnp.concatenate([packed[h:, :h], packed[h:, h:]], 0)
    return jnp.concatenate(
        [jnp.concatenate([packed[:h, :h], low.T], 1), jnp.concatenate([low, packed[:h, h:]], 1)], 0
    )


def quarters(leaf, n, a, b):
    h = n // 2

    def block(row, rows, col):
        return leaf.at[pl.ds(pl.multiple_of(a * n + row, h // 2), rows), pl.ds(pl.multiple_of(b * n + col, h), h)]

    return block


def fetch(moves, sems):
    copies = [pltpu.make_async_copy(a, b, sems.at[k]) for k, (a, b) in enumerate(moves)]
    for copy in copies:
        copy.start()
    for copy in copies:
        copy.wait()


def symmetric(leaf, e, out, base):
    n = out.shape[1]
    h = n // 2
    block = quarters(leaf, n, e, e)
    return [
        (block(0, h, 0), out.at[pl.ds(base, h), pl.ds(0, h)]),
        (block(h, h, h), out.at[pl.ds(base, h), pl.ds(h, h)]),
        (block(h, h // 2, 0), out.at[pl.ds(base + h, h // 2), pl.ds(0, h)]),
        (block(h + h // 2, h // 2, 0), out.at[pl.ds(base + h, h // 2), pl.ds(h, h)]),
    ]


def passing_kernel(middle, middle_z, out):
    n = out.shape[1]
    out[:n] = middle_z[:n]
    out[n:] = middle[n:] + middle_z[n:]


def relay_kernel(given, out):
    out[...] = given[...]


def sum_kernel(own, other, out):
    out[...] = own[...] + other[...]


def outer_rows(leaf, edge, rows, sems):
    n = rows.shape[0]
    _, x, _, d = edges()
    own = pl.ds(pl.multiple_of(edge * n, n), n)
    return [
        pltpu.make_async_copy(leaf.at[own, pl.ds(pl.multiple_of(e * n, n), n)], rows.at[:, pl.ds(p * n, n)], sems.at[p])
        for p, e in enumerate((x, d))
    ]


def side_kernel(base, leaf, data, out, rows, held, sems):
    n, width = rows.shape[0], held.shape[1]
    i, _, y, _ = edges()
    copies = outer_rows(leaf, i, rows, sems)
    copies.append(pltpu.make_async_copy(data.at[:, pl.ds(base, width)], held, sems.at[2]))
    for copy in copies:
        copy.start()
    if out.shape[1] > width:
        whole = leaf.at[pl.ds(pl.multiple_of(y * n, n), n), pl.ds(pl.multiple_of(i * n, n), n)]
        fetch([(whole, out.at[:, pl.ds(width, n)])], sems.at[pl.ds(3, 1)])
    for copy in copies:
        copy.wait()
    out[:, :width] = triple(split(rows[...]), split(held[...]))


def blocks_kernel(leaf, joined, middle, sems):
    n = joined.shape[1]
    i, _, y, _ = edges()
    whole = leaf.at[pl.ds(pl.multiple_of(y * n, n), n), pl.ds(pl.multiple_of(i * n, n), n)]
    fetch([(whole, middle.at[pl.ds(0, n)])] + symmetric(leaf, y, middle, n) + symmetric(leaf, i, joined, 0), sems)


def passing_kernel(middle, middle_z, out):
    n = out.shape[1]
    out[:n] = middle_z[:n]
    out[n:] = middle[n:] + middle_z[n:]


def relay_kernel(given, out):
    out[...] = given[...]


def sum_kernel(own, other, out):
    out[...] = own[...] + other[...]


def append_kernel(before, own, other, out):
    width = before.shape[1]
    out[:, :width] = before[...]
    out[:, width:] = own[...] + other[...]


def outer_rows(leaf, edge, rows, sems):
    n = rows.shape[0]
    _, x, _, d = edges()
    own = pl.ds(pl.multiple_of(edge * n, n), n)
    return [
        pltpu.make_async_copy(leaf.at[own, pl.ds(pl.multiple_of(e * n, n), n)], rows.at[:, pl.ds(p * n, n)], sems.at[p])
        for p, e in enumerate((x, d))
    ]


def side_kernel(base, leaf, data, out, rows, held, sems):
    n, width = rows.shape[0], held.shape[1]
    i, _, y, _ = edges()
    copies = outer_rows(leaf, i, rows, sems)
    copies.append(pltpu.make_async_copy(data.at[:, pl.ds(base, width)], held, sems.at[2]))
    for copy in copies:
        copy.start()
    if out.shape[1] > width:
        whole = leaf.at[pl.ds(pl.multiple_of(y * n, n), n), pl.ds(pl.multiple_of(i * n, n), n)]
        fetch([(whole, out.at[:, pl.ds(width, n)])], sems.at[pl.ds(3, 1)])
    for copy in copies:
        copy.wait()
    out[:, :width] = triple(split(rows[...]), split(held[...]))


def joined_kernel(leaf, out, sems):
    fetch(symmetric(leaf, edges()[0], out, 0), sems)


def crossing_kernel(leaf, out, sems):
    n = out.shape[1]
    i, _, y, _ = edges()
    whole = leaf.at[pl.ds(pl.multiple_of(y * n, n), n), pl.ds(pl.multiple_of(i * n, n), n)]
    fetch([(whole, out.at[pl.ds(0, n)])] + symmetric(leaf, y, out, n), sems)


def known_kernel(leaf, data, flux, high, low, potential, _, data_high, data_low, sems):
    step = pl.program_id(0)
    n = leaf.shape[0]
    i, x, y, d = edges()
    copies = [
        pltpu.make_async_copy(data.at[pl.ds(p * n, n), :], potential.at[pl.ds(pl.multiple_of(e * n, n), n), :], sems.at[p])
        for p, e in enumerate((x, d))
    ]

    @pl.when(step == 0)
    def _():
        for copy in copies:
            copy.start()
        data_high[...], data_low[...] = split(data[...])

    cols = lambda e: leaf[:, pl.ds(pl.multiple_of(e * n, n), n)]
    unknown = split(jnp.concatenate([cols(i), cols(y)], 1))
    high[...], low[...] = unknown
    outer = split(jnp.concatenate([cols(x), cols(d)], 1))
    flux[...] = triple(outer, (data_high[...], data_low[...]))

    @pl.when(step == pl.num_programs(0) - 1)
    def _():
        for copy in copies:
            copy.wait()


def first_kernel(joined, joined_far, middle, inverse, across, half):
    n = inverse.shape[0]
    h = n // 2
    solved = invert(unpack(joined[...] + joined_far[...]))
    inverse[...] = solved
    across[...] = near_nt(solved, middle[:n])

    def fill(diagonal, low):
        half[:h] = diagonal
        half[h:] = low

    @pl.when(side("gx") == 0)
    def _():
        fill(solved[:h, :h], solved[h : h + h // 2, :h])

    @pl.when(side("gx") == 1)
    def _():
        fill(solved[h:, h:], solved[h + h // 2 :, :h])


def middle_kernel(base, offset, widths, leaf, data, own, far, across, inverse, *rest):
    outs, (start, rows, held, sems) = rest[:-4], rest[-4:]
    width = sum(widths)
    copies = outer_rows(leaf, edges()[2], rows, sems)
    copies.append(pltpu.make_async_copy(data.at[:, pl.ds(base, width)], held, sems.at[2]))
    for copy in copies:
        copy.start()
    right = split(own[:, offset : offset + width] + far[:, offset : offset + width])
    start[...] = -triple(split(inverse[...]), right)
    out = triple(split(across[...].T), right)
    for copy in copies:
        copy.wait()
    out = triple(split(rows[...]), split(held[...])) - out
    done = 0
    for ref, part in zip(outs, widths):
        ref[...] = out[:, done : done + part]
        done += part


def build_kernel(middle, middle_z, passed, side_far, inverse, half_z, half_x, across, across_far, own, off, far, other):
    n = inverse.shape[0]
    h = n // 2

    def fill(one, two):
        low = jnp.concatenate([one[h:], two[h:]], 0)
        other[:h, :h] = one[:h]
        other[h:, h:] = two[:h]
        other[h:, :h] = low
        other[:h, h:] = low.T

    @pl.when(side("gx") == 0)
    def _():
        fill(half_z, half_x)

    @pl.when(side("gx") == 1)
    def _():
        fill(half_x, half_z)

    cross = side_far[:, -n:]
    q_far = near_nt(inverse[...], cross)
    q_own = across[...]
    across_far[...] = q_far
    p_own = near_nt(other[...], middle_z[:n])
    p_far = near_nt(other[...], passed[:n])
    own[...] = unpack(middle[n:] + middle_z[n:]) - (near_nn(middle[:n], q_own) + near_nn(middle_z[:n], p_own))
    off[...] = -(near_nn(middle[:n], q_far) + near_nn(middle_z[:n], p_far))
    far[...] = unpack(passed[n:]) - (near_nn(cross, q_far) + near_nn(passed[:n], p_far))


def open_half(matrix, head, reach, rest):
    h = matrix.shape[0] // 2
    solved = invert(matrix[:h, :h])
    head[...] = solved
    reach[...] = full_nn(solved, matrix[:h, h:])
    rest[...] = matrix[h:, h:] - full_tn(matrix[:h, h:], reach[...])


def head_kernel(matrix, head, reach, rest):
    open_half(matrix, head, reach, rest)


def turn_kernel(head, reach, rest, off, far, done, wide, left):
    done[...] = join(head[...], reach[...], invert(rest[...]))
    wide[...] = near_nn(done[...], off[...])
    left[...] = far[...] - near_tn(off[...], wide[...])


def tail_kernel(head, reach, rest, done, wide, across, across_far, high, low):
    n = done.shape[0]
    solved = near_join(done[...], wide[...], join(head[...], reach[...], invert(rest[...])))
    inward = triple(split(jnp.concatenate([across[...], across_far[...]], 1)), split(solved))
    high[...], low[...] = split(jnp.concatenate([inward, -solved[:n]], 0))


def last_kernel(count, base, solve_high, solve_low, high, low, known, *rest):
    w_own, w_far, starts = rest[:count], rest[count : 2 * count], rest[2 * count : -7]
    flux, potential, solved, made, sems = rest[-5:]
    n, width = w_own[0].shape[0], solved.shape[1]
    i, _, y, _ = edges()
    cols = pl.ds(base, width)
    tops, rests, done = [], [], 0
    shift = jnp.concatenate([start[...] for start in starts], 1)
    for own, far in zip(w_own, w_far):
        part = slice(done, done + own.shape[1])
        inner = triple((solve_high[...], solve_low[...]), split(jnp.concatenate([own[...], far[...]], 0)))
        tops.append(inner[:n] + shift[:, part])
        rests.append(inner[n:])
        done = part.stop
    values = jnp.concatenate([jnp.concatenate(tops, 1), jnp.concatenate(rests, 1)], 0)
    solved[...] = values
    copies = []
    for p, e in enumerate((i, y)):
        rows = pl.ds(pl.multiple_of(e * n, n), n)
        copies.append(pltpu.make_async_copy(solved.at[pl.ds(p * n, n), :], potential.at[rows, cols], sems.at[4 + p]))
        copies[-1].start()
    right = split(values)
    for k in range(4):
        rows = pl.ds(k * n, n)
        made[rows] = known[rows, base : base + width] + triple((high[rows], low[rows]), right)
        copies.append(pltpu.make_async_copy(made.at[rows], flux.at[rows, cols], sems.at[k]))
        copies[-1].start()
    for copy in copies:
        copy.wait()


def array(*shape, dtype=F32):
    return jax.ShapeDtypeStruct(shape, dtype)


ANY = pl.BlockSpec(memory_space=pl.ANY)
HBM = pl.BlockSpec(memory_space=pltpu.HBM)
WHOLE = pl.BlockSpec(memory_space=pltpu.VMEM)
MIB = 1 << 20
EARLY = 58


COSTS = {
    "passing": 8.0,
    "relay": 8.0,
    "build": 0.7,
    "opening": 1.2,
    "copy": 0.05,
    "closing": 0.3,
}


class Chain:
    def __init__(self):
        self.mark = None

    def __call__(self, name, kernel, outs, *args, ins=None, out_specs=None, scratch=(), aliases=None, limit=24, **kwargs):
        cost = COSTS.get(name, 0.005)
        ins = ins or [WHOLE] * len(args)
        out_specs = out_specs or [WHOLE] * len(outs)
        marks = [] if self.mark is None else [self.mark]

        def body(*refs):
            inner = refs[: len(args)] + refs[len(args) + len(marks) :]
            kernel(*inner[: len(args) + len(outs)], *inner[len(args) + len(outs) + 1 :])

        *given, self.mark = pl.pallas_call(
            body,
            out_shape=list(outs) + [array(8, LANES)],
            in_specs=list(ins) + [HBM] * len(marks),
            out_specs=list(out_specs) + [HBM],
            scratch_shapes=list(scratch),
            input_output_aliases=aliases or {},
            compiler_params=pltpu.CompilerParams(vmem_limit_bytes=limit * MIB),
            cost_estimate=pl.CostEstimate(flops=int(cost * 1e9), bytes_accessed=int(cost * 3e6), transcendentals=0),
            name=name,
            **kwargs,
        )(*args, *marks)
        return given[0] if len(given) == 1 else given


def per_device(leaf_maps, edge_data):
    leaf = leaf_maps[0, 0]
    data = edge_data[0, 0]
    full, count = leaf.shape[0], data.shape[1]
    n = full // 4
    h = n // 2
    packed = 3 * n // 4
    dma = pltpu.SemaphoreType.DMA
    call = Chain()
    unit = count // 8
    widths = [2 * unit] * 4
    bases = [0, 2 * unit, 4 * unit, 6 * unit]

    joined, middle = call(
        "blocks",
        blocks_kernel,
        [array(packed, n), array(n + packed, n)],
        leaf,
        limit=EARLY,
        ins=[HBM],
        scratch=[dma((9,))],
    )
    middle_z = exchange(middle, "gy")
    joined_far = exchange(joined, "gx")

    def sides(base, width, extra=0):
        own = call(
            "side",
            functools.partial(side_kernel, base),
            [array(n, width + extra)],
            leaf,
            data,
            ins=[HBM] * 2,
            scratch=[pltpu.VMEM((n, 2 * n), F32), pltpu.VMEM((2 * n, width), F32), dma((4,))],
        )
        return own, exchange(own, "gx")

    def middles(parts, offset, own, far):
        base, width = bases[parts[0]], sum(widths[k] for k in parts)
        given = call(
            "middle",
            functools.partial(middle_kernel, base, base - offset, [widths[k] for k in parts]),
            [array(n, widths[k]) for k in parts] + [array(n, width)],
            leaf,
            data,
            own,
            far,
            across,
            inverse1,
            ins=[ANY] * 2 + [WHOLE] * 4,
            scratch=[pltpu.VMEM((n, 2 * n), F32), pltpu.VMEM((2 * n, width), F32), dma((3,))],
        )
        return given[:-1], given[-1]

    def total(own, far, name="total"):
        w = call(name, sum_kernel, [array(*own.shape)], own, far)
        return w, exchange(w, "gx")

    def copy(given, name="copy"):
        return call(name, relay_kernel, [array(*given.shape)], given)

    own_a, far_a = sides(0, 4 * unit, n)
    inverse1, across, half = call(
        "first", first_kernel, [array(n, n)] * 2 + [array(packed, h)], joined, joined_far, middle
    )
    half_z = exchange(half, "gy")
    known, high, low, potential, flux = call(
        "known",
        known_kernel,
        [
            array(full, count),
            array(full, 2 * n, dtype=BF16),
            array(full, 2 * n, dtype=BF16),
            array(full, count),
            array(full, count),
        ],
        leaf,
        data,
        ins=[pl.BlockSpec((n, full), lambda s: (s, 0)), pl.BlockSpec((2 * n, count), lambda s: (0, 0))],
        out_specs=[
            pl.BlockSpec((n, count), lambda s: (s, 0)),
            pl.BlockSpec((n, 2 * n), lambda s: (s, 0)),
            pl.BlockSpec((n, 2 * n), lambda s: (s, 0)),
            ANY,
            ANY,
        ],
        scratch=[pltpu.VMEM((2 * n, count), BF16), pltpu.VMEM((2 * n, count), BF16), dma((2,))],
        grid=(4,),
    )
    passing = call("passing", passing_kernel, [array(n + packed, n)], middle, middle_z)
    passed = exchange(passing, "gx")
    (v0,), start0 = middles([0], 0, own_a, far_a)
    z0 = exchange(v0, "gy")
    half_z = copy(half_z, "relay")
    half_x = exchange(half_z, "gx")
    (v1,), start1 = middles([1], 0, own_a, far_a)
    z1 = exchange(v1, "gy")
    own_b, far_b = sides(bases[2], widths[2])
    across_far, s_own, s_off, s_far = call(
        "build",
        build_kernel,
        [array(n, n)] * 4,
        middle,
        middle_z,
        passed,
        far_a,
        inverse1,
        half_z,
        half_x,
        across,
        scratch=[pltpu.VMEM((n, n), F32)],
    )
    own_c, far_c = sides(bases[3], 2 * unit)
    head, reach, rest = call("head", head_kernel, [array(h, h)] * 3, s_own)
    w0, w0_far = total(v0, z0, "opening")
    (v2,), start2 = middles([2], bases[2], own_b, far_b)
    z2 = exchange(v2, "gy")
    done, wide, left = call("turn", turn_kernel, [array(n, n)] * 3, head, reach, rest, s_off, s_far)
    w1, w1_far = total(v1, z1)
    (v3,), start3 = middles([3], bases[3], own_c, far_c)
    z3 = exchange(v3, "gy")
    head, reach, rest = call("head", head_kernel, [array(h, h)] * 3, left)
    w2, w2_far = total(v2, z2)
    inverse2 = call(
        "tail", tail_kernel, [array(2 * n, 2 * n, dtype=BF16)] * 2, head, reach, rest, done, wide, across, across_far
    )

    def last(base, own, far, starts, held):
        width = sum(part.shape[1] for part in own)
        fixed = 5 + 2 * len(own) + len(starts)
        return call(
            "last",
            functools.partial(last_kernel, len(own), base),
            [array(full, count), array(full, count)],
            *inverse2,
            high,
            low,
            known,
            *own,
            *far,
            *starts,
            *held[1:],
            *held[:1],
            ins=[WHOLE] * fixed + [ANY] * len(held),
            out_specs=[ANY] * 2,
            scratch=[pltpu.VMEM((2 * n, width), F32), pltpu.VMEM((full, width), F32), dma((6,))],
            aliases={fixed: 1, fixed + 1: 0},
        )

    w3, w3_far = total(v3, z3, "closing")
    w0_far = copy(w0_far)
    held = last(0, [w0, w1, w2], [w0_far, w1_far, w2_far], [start0, start1, start2], [flux, potential])
    held = last(bases[3], [w3], [w3_far], [start3], held)
    return held[1][None, None], held[0][None, None]


def solution(mesh):
    spec = P("gx", "gy", None, None)
    return jax.shard_map(per_device, mesh=mesh, in_specs=(spec, spec), out_specs=(spec, spec), check_vma=False)
```

```python
import functools

import jax
import jax.numpy as jnp
from jax import lax
from jax.experimental import pallas as pl
from jax.experimental.pallas import tpu as pltpu
from jax.sharding import PartitionSpec as P

HIGHEST = lax.Precision.HIGHEST
F32 = jnp.float32
BF16 = jnp.bfloat16
LANES = 128
PANEL = 8
TURN = 8


def exchange(block, axis):
    half = lax.axis_size(axis) // 2
    return lax.ppermute(block, axis, [(i, i ^ half) for i in range(2 * half)])


def side(axis):
    return (lax.axis_index(axis) >= lax.axis_size(axis) // 2).astype(jnp.int32)


def edges():
    c, r = side("gx"), side("gy")
    return 1 - c, c, 3 - r, 2 + r


def contract(left, right, dims):
    return lax.dot_general(left, right, ((dims[:1], dims[1:]), ((), ())), precision=HIGHEST, preferred_element_type=F32)


def full_nn(left, right):
    return contract(left, right, (1, 0))


def full_nt(left, right):
    return contract(left, right, (1, 1))


def full_tn(left, right):
    return contract(left, right, (0, 0))


def split(values):
    high = values.astype(BF16)
    return high, (values - high.astype(F32)).astype(BF16)


def half_dot(left, right):
    return jnp.dot(left, right, preferred_element_type=F32)


def triple(left, right):
    (lh, ll), (rh, rl) = left, right
    return half_dot(lh, rh) + (half_dot(lh, rl) + half_dot(ll, rh))


def near_nn(left, right):
    return triple(split(left), split(right))


def near_nt(left, right):
    return near_nn(left, right.T)


def near_tn(left, right):
    return near_nn(left.T, right)


def tree(terms):
    while len(terms) > 1:
        terms = [a + b for a, b in zip(terms[::2], terms[1::2])]
    return terms[0]


def entry(i, j):
    return (i, j) if i >= j else (j, i)


def invert_panel(s):
    s = dict(s)
    for k in range(PANEL):
        inverse = 1.0 / s[k, k]
        rest = [i for i in range(PANEL) if i != k]
        column = {i: s[entry(i, k)] for i in rest}
        scaled = {i: column[i] * inverse for i in rest}
        for i in rest:
            for j in rest:
                if j <= i:
                    s[i, j] = s[i, j] - scaled[i] * column[j]
        for i in rest:
            s[entry(i, k)] = scaled[i]
        s[k, k] = -inverse
    return {key: -value for key, value in s.items()}


def invert_tile(tile):
    shape = (PANEL, LANES)
    lane = lax.broadcasted_iota(jnp.int32, shape, 1)
    sub = lax.broadcasted_iota(jnp.int32, shape, 0)
    count = LANES // PANEL

    def turn(_, rows):
        rows = list(rows)
        for q in range(TURN):
            start = PANEL * q
            panel = rows[q]
            columns = [jnp.broadcast_to(panel[:, start + j : start + j + 1], shape) for j in range(PANEL)]
            s = {(i, j): jnp.broadcast_to(columns[j][i : i + 1, :], shape) for i in range(PANEL) for j in range(i + 1)}
            inverse = invert_panel(s)
            inside = (lane >= start) & (lane < start + PANEL)
            unit = jnp.where(inside, jnp.where(lane - start == sub, 1.0, 0.0), panel)
            wide = [jnp.broadcast_to(unit[j : j + 1, :], shape) for j in range(PANEL)]
            swept = [tree([inverse[entry(i, j)] * wide[j] for j in range(PANEL)]) for i in range(PANEL)]
            new = swept[0]
            for i in range(1, PANEL):
                new = jnp.where(sub == i, swept[i], new)
            for p in [*range(q + 1, count), *range(q)]:
                row = rows[p]
                terms = [jnp.broadcast_to(row[:, start + j : start + j + 1], shape) * swept[j] for j in range(PANEL)]
                rows[p] = jnp.where(inside, 0.0, row) - tree(terms)
            rows[q] = new
        return tuple(pltpu.roll(row, LANES - PANEL * TURN, 1) for row in rows[TURN:] + rows[:TURN])

    rows = tuple(tile[PANEL * i : PANEL * (i + 1), :] for i in range(count))
    return jnp.concatenate(lax.fori_loop(0, count // TURN, turn, rows), 0)


def invert(matrix):
    size = matrix.shape[0]
    if size == LANES:
        return invert_tile(matrix)
    half = size // 2
    first, cross, last = matrix[:half, :half], matrix[:half, half:], matrix[half:, half:]
    head = invert(first)
    reach = full_nn(head, cross)
    tail = invert(last - full_tn(cross, reach))
    return join(head, reach, tail)


def join(head, reach, tail):
    corner = full_nn(reach, tail)
    top = jnp.concatenate([head + full_nt(corner, reach), -corner], 1)
    return jnp.concatenate([top, jnp.concatenate([-corner.T, tail], 1)], 0)


def near_join(head, reach, tail):
    corner = near_nn(reach, tail)
    top = jnp.concatenate([head + near_nt(corner, reach), -corner], 1)
    return jnp.concatenate([top, jnp.concatenate([-corner.T, tail], 1)], 0)


def unpack(packed):
    h = packed.shape[1] // 2
    low = jnp.concatenate([packed[h:, :h], packed[h:, h:]], 0)
    return jnp.concatenate(
        [jnp.concatenate([packed[:h, :h], low.T], 1), jnp.concatenate([low, packed[:h, h:]], 1)], 0
    )


def fold(square):
    h = square.shape[0] // 2
    low = square[h:, :h]
    top = jnp.concatenate([square[:h, :h], square[h:, h:]], 1)
    return jnp.concatenate([top, jnp.concatenate([low[: h // 2], low[h // 2 :]], 1)], 0)


def fold_twice(square):
    h = square.shape[0] // 2
    once = fold(square)
    top = jnp.concatenate([fold(once[:h, :h]), fold(once[:h, h:])], 1)
    return jnp.concatenate([top, once[h:]], 0)


def unfold_twice(packed):
    h = packed.shape[1] // 2
    tall = 3 * h // 4
    top = jnp.concatenate([unpack(packed[:tall, :h]), unpack(packed[:tall, h:])], 1)
    return unpack(jnp.concatenate([top, packed[tall:]], 0))


def quarters(leaf, n, a, b):
    h = n // 2

    def block(row, rows, col):
        return leaf.at[pl.ds(pl.multiple_of(a * n + row, h // 2), rows), pl.ds(pl.multiple_of(b * n + col, h), h)]

    return block


def fetch(moves, sems):
    copies = [pltpu.make_async_copy(a, b, sems.at[k]) for k, (a, b) in enumerate(moves)]
    for copy in copies:
        copy.start()
    for copy in copies:
        copy.wait()


def symmetric(leaf, e, out, base):
    n = out.shape[1]
    h = n // 2
    block = quarters(leaf, n, e, e)
    return [
        (block(0, h, 0), out.at[pl.ds(base, h), pl.ds(0, h)]),
        (block(h, h, h), out.at[pl.ds(base, h), pl.ds(h, h)]),
        (block(h, h // 2, 0), out.at[pl.ds(base + h, h // 2), pl.ds(0, h)]),
        (block(h + h // 2, h // 2, 0), out.at[pl.ds(base + h, h // 2), pl.ds(h, h)]),
    ]


def blocks_kernel(leaf, joined, middle, held, sems):
    n = joined.shape[1]
    i, _, y, _ = edges()
    block = lambda a, b: leaf.at[pl.ds(pl.multiple_of(a * n, n), n), pl.ds(pl.multiple_of(b * n, n), n)]
    fetch([(block(y, y), held), (block(y, i), middle.at[pl.ds(0, n)])] + symmetric(leaf, i, joined, 0), sems)
    middle[n:] = fold_twice(held[...])


def passing_kernel(middle, middle_z, out):
    n = out.shape[1]
    out[:n] = middle_z[:n]
    out[n:] = middle[n:] + middle_z[n:]


def relay_kernel(given, out):
    out[...] = given[...]


def sum_kernel(own, other, out):
    out[...] = own[...] + other[...]


def outer_rows(leaf, edge, rows, sems):
    n = rows.shape[0]
    _, x, _, d = edges()
    own = pl.ds(pl.multiple_of(edge * n, n), n)
    return [
        pltpu.make_async_copy(leaf.at[own, pl.ds(pl.multiple_of(e * n, n), n)], rows.at[:, pl.ds(p * n, n)], sems.at[p])
        for p, e in enumerate((x, d))
    ]


def side_kernel(base, leaf, data, out, rows, held, sems):
    n, width = rows.shape[0], held.shape[1]
    i, _, y, _ = edges()
    copies = outer_rows(leaf, i, rows, sems)
    copies.append(pltpu.make_async_copy(data.at[:, pl.ds(base, width)], held, sems.at[2]))
    for copy in copies:
        copy.start()
    if out.shape[1] > width:
        whole = leaf.at[pl.ds(pl.multiple_of(y * n, n), n), pl.ds(pl.multiple_of(i * n, n), n)]
        fetch([(whole, out.at[:, pl.ds(width, n)])], sems.at[pl.ds(3, 1)])
    for copy in copies:
        copy.wait()
    out[:, :width] = triple(split(rows[...]), split(held[...]))


def known_kernel(leaf, data, flux, high, low, data_high, data_low):
    n = leaf.shape[0]
    i, x, y, d = edges()

    @pl.when(pl.program_id(0) == 0)
    def _():
        data_high[...], data_low[...] = split(data[...])

    cols = lambda e: leaf[:, pl.ds(pl.multiple_of(e * n, n), n)]
    high[...], low[...] = split(jnp.concatenate([cols(i), cols(y)], 1))
    outer = split(jnp.concatenate([cols(x), cols(d)], 1))
    flux[...] = triple(outer, (data_high[...], data_low[...]))


def known_and_data_kernel(leaf, data, flux, high, low, potential, _, data_high, data_low, sems):
    n = leaf.shape[0]
    _, x, _, d = edges()
    copies = [
        pltpu.make_async_copy(data.at[pl.ds(p * n, n), :], potential.at[pl.ds(pl.multiple_of(e * n, n), n), :], sems.at[p])
        for p, e in enumerate((x, d))
    ]

    @pl.when(pl.program_id(0) == 0)
    def _():
        for copy in copies:
            copy.start()

    known_kernel(leaf, data, flux, high, low, data_high, data_low)

    @pl.when(pl.program_id(0) == pl.num_programs(0) - 1)
    def _():
        for copy in copies:
            copy.wait()


def first_kernel(joined, joined_far, middle, inverse, across, half):
    n = inverse.shape[0]
    h = n // 2
    solved = invert(unpack(joined[...] + joined_far[...]))
    inverse[...] = solved
    across[...] = near_nt(solved, middle[:n])

    def fill(diagonal, low):
        half[:h] = diagonal
        half[h:] = low

    @pl.when(side("gx") == 0)
    def _():
        fill(solved[:h, :h], solved[h : h + h // 2, :h])

    @pl.when(side("gx") == 1)
    def _():
        fill(solved[h:, h:], solved[h + h // 2 :, :h])


def middle_kernel(base, offset, widths, leaf, data, own, far, across, inverse, *rest):
    outs, (start, rows, held, sems) = rest[:-4], rest[-4:]
    width = sum(widths)
    copies = outer_rows(leaf, edges()[2], rows, sems)
    copies.append(pltpu.make_async_copy(data.at[:, pl.ds(base, width)], held, sems.at[2]))
    for copy in copies:
        copy.start()
    right = split(own[:, offset : offset + width] + far[:, offset : offset + width])
    start[...] = -triple(split(inverse[...]), right)
    out = triple(split(across[...].T), right)
    for copy in copies:
        copy.wait()
    out = triple(split(rows[...]), split(held[...])) - out
    done = 0
    for ref, part in zip(outs, widths):
        ref[...] = out[:, done : done + part]
        done += part


def build_kernel(middle, middle_z, passed, side_far, inverse, half_z, half_x, across, across_far, own, off, far, other):
    n = inverse.shape[0]
    h = n // 2

    def fill(one, two):
        low = jnp.concatenate([one[h:], two[h:]], 0)
        other[:h, :h] = one[:h]
        other[h:, h:] = two[:h]
        other[h:, :h] = low
        other[:h, h:] = low.T

    @pl.when(side("gx") == 0)
    def _():
        fill(half_z, half_x)

    @pl.when(side("gx") == 1)
    def _():
        fill(half_x, half_z)

    cross = side_far[:, -n:]
    q_far = near_nt(inverse[...], cross)
    q_own = across[...]
    across_far[...] = q_far
    p_own = near_nt(other[...], middle_z[:n])
    p_far = near_nt(other[...], passed[:n])
    own[...] = unfold_twice(middle[n:] + middle_z[n:]) - (near_nn(middle[:n], q_own) + near_nn(middle_z[:n], p_own))
    off[...] = -(near_nn(middle[:n], q_far) + near_nn(middle_z[:n], p_far))
    far[...] = unfold_twice(passed[n:]) - (near_nn(cross, q_far) + near_nn(passed[:n], p_far))


def open_half(matrix, head, reach, rest):
    h = matrix.shape[0] // 2
    solved = invert(matrix[:h, :h])
    head[...] = solved
    reach[...] = full_nn(solved, matrix[:h, h:])
    rest[...] = matrix[h:, h:] - full_tn(matrix[:h, h:], reach[...])


def head_kernel(matrix, head, reach, rest):
    open_half(matrix, head, reach, rest)


def turn_kernel(head, reach, rest, off, far, done, wide, left):
    done[...] = join(head[...], reach[...], invert(rest[...]))
    wide[...] = near_nn(done[...], off[...])
    left[...] = far[...] - near_tn(off[...], wide[...])


def tail_kernel(head, reach, rest, done, wide, across, across_far, high, low):
    n = done.shape[0]
    solved = near_join(done[...], wide[...], join(head[...], reach[...], invert(rest[...])))
    inward = triple(split(jnp.concatenate([across[...], across_far[...]], 1)), split(solved))
    high[...], low[...] = split(jnp.concatenate([inward, -solved[:n]], 0))


def last_kernel(count, base, solve_high, solve_low, *rest):
    halves, rest = (rest[:3], rest[3:6]), rest[6:]
    w_own, w_far, starts = rest[:count], rest[count : 2 * count], rest[2 * count : -7]
    flux, potential, solved, made, sems = rest[-5:]
    n, width = w_own[0].shape[0], solved.shape[1]
    i, _, y, _ = edges()
    cols = pl.ds(base, width)
    tops, rests, done = [], [], 0
    shift = jnp.concatenate([start[...] for start in starts], 1)
    for own, far in zip(w_own, w_far):
        part = slice(done, done + own.shape[1])
        inner = triple((solve_high[...], solve_low[...]), split(jnp.concatenate([own[...], far[...]], 0)))
        tops.append(inner[:n] + shift[:, part])
        rests.append(inner[n:])
        done = part.stop
    values = jnp.concatenate([jnp.concatenate(tops, 1), jnp.concatenate(rests, 1)], 0)
    solved[...] = values
    copies = []
    for p, e in enumerate((i, y)):
        rows = pl.ds(pl.multiple_of(e * n, n), n)
        copies.append(pltpu.make_async_copy(solved.at[pl.ds(p * n, n), :], potential.at[rows, cols], sems.at[4 + p]))
        copies[-1].start()
    right = split(values)
    for k in range(4):
        rows = pl.ds(k * n, n)
        known, high, low = (ref.at[pl.ds(k % 2 * n, n)] for ref in halves[k // 2])
        made[rows] = known[:, base : base + width] + triple((high[...], low[...]), right)
        copies.append(pltpu.make_async_copy(made.at[rows], flux.at[rows, cols], sems.at[k]))
        copies[-1].start()
    for copy in copies:
        copy.wait()


def array(*shape, dtype=F32):
    return jax.ShapeDtypeStruct(shape, dtype)


ANY = pl.BlockSpec(memory_space=pl.ANY)
HBM = pl.BlockSpec(memory_space=pltpu.HBM)
WHOLE = pl.BlockSpec(memory_space=pltpu.VMEM)
MIB = 1 << 20
EARLY = 58


COSTS = {
    "passing": 8.0,
    "relay": 8.0,
    "build": 0.7,
    "opening": 1.2,
    "copy": 0.05,
    "closing": 0.3,
}


class Chain:
    def __init__(self):
        self.mark = None

    def __call__(self, name, kernel, outs, *args, ins=None, out_specs=None, scratch=(), aliases=None, limit=24, **kwargs):
        cost = COSTS.get(name, 0.005)
        ins = ins or [WHOLE] * len(args)
        out_specs = out_specs or [WHOLE] * len(outs)
        marks = [] if self.mark is None else [self.mark]

        def body(*refs):
            inner = refs[: len(args)] + refs[len(args) + len(marks) :]
            kernel(*inner[: len(args) + len(outs)], *inner[len(args) + len(outs) + 1 :])

        *given, self.mark = pl.pallas_call(
            body,
            out_shape=list(outs) + [array(8, LANES)],
            in_specs=list(ins) + [HBM] * len(marks),
            out_specs=list(out_specs) + [HBM],
            scratch_shapes=list(scratch),
            input_output_aliases=aliases or {},
            compiler_params=pltpu.CompilerParams(vmem_limit_bytes=limit * MIB),
            cost_estimate=pl.CostEstimate(flops=int(cost * 1e9), bytes_accessed=int(cost * 3e6), transcendentals=0),
            name=name,
            **kwargs,
        )(*args, *marks)
        return given[0] if len(given) == 1 else given


def per_device(leaf_maps, edge_data):
    leaf = leaf_maps[0, 0]
    data = edge_data[0, 0]
    full, count = leaf.shape[0], data.shape[1]
    n = full // 4
    h = n // 2
    packed = 3 * n // 4
    tight = 5 * n // 8
    dma = pltpu.SemaphoreType.DMA
    call = Chain()
    unit = count // 8
    widths = [2 * unit] * 4
    bases = [0, 2 * unit, 4 * unit, 6 * unit]

    joined, middle = call(
        "blocks",
        blocks_kernel,
        [array(packed, n), array(n + tight, n)],
        leaf,
        limit=EARLY,
        ins=[HBM],
        scratch=[pltpu.VMEM((n, n), F32), dma((6,))],
    )
    middle_z = exchange(middle, "gy")
    joined_far = exchange(joined, "gx")

    def sides(base, width, extra=0):
        own = call(
            "side",
            functools.partial(side_kernel, base),
            [array(n, width + extra)],
            leaf,
            data,
            ins=[HBM] * 2,
            scratch=[pltpu.VMEM((n, 2 * n), F32), pltpu.VMEM((2 * n, width), F32), dma((4,))],
        )
        return own, exchange(own, "gx")

    def middles(parts, offset, own, far):
        base, width = bases[parts[0]], sum(widths[k] for k in parts)
        given = call(
            "middle",
            functools.partial(middle_kernel, base, base - offset, [widths[k] for k in parts]),
            [array(n, widths[k]) for k in parts] + [array(n, width)],
            leaf,
            data,
            own,
            far,
            across,
            inverse1,
            ins=[ANY] * 2 + [WHOLE] * 4,
            scratch=[pltpu.VMEM((n, 2 * n), F32), pltpu.VMEM((2 * n, width), F32), dma((3,))],
        )
        return given[:-1], given[-1]

    def total(own, far, name="total"):
        w = call(name, sum_kernel, [array(*own.shape)], own, far)
        return w, exchange(w, "gx")

    def copy(given, name="copy"):
        return call(name, relay_kernel, [array(*given.shape)], given)

    own_a, far_a = sides(0, 4 * unit, n)
    inverse1, across, half = call(
        "first", first_kernel, [array(n, n)] * 2 + [array(packed, h)], joined, joined_far, middle
    )
    half_z = exchange(half, "gy")
    def known_half(name, kernel, first, outs, out_specs, sems):
        return call(
            name,
            kernel,
            [array(2 * n, count), array(2 * n, 2 * n, dtype=BF16), array(2 * n, 2 * n, dtype=BF16), *outs],
            leaf,
            data,
            ins=[pl.BlockSpec((n, full), lambda s: (s + first, 0)), pl.BlockSpec((2 * n, count), lambda s: (0, 0))],
            out_specs=[
                pl.BlockSpec((n, count), lambda s: (s, 0)),
                pl.BlockSpec((n, 2 * n), lambda s: (s, 0)),
                pl.BlockSpec((n, 2 * n), lambda s: (s, 0)),
                *out_specs,
            ],
            scratch=[pltpu.VMEM((2 * n, count), BF16), pltpu.VMEM((2 * n, count), BF16), *sems],
            grid=(2,),
        )

    *known_a, potential, flux = known_half(
        "known_and_data", known_and_data_kernel, 0, [array(full, count)] * 2, [ANY] * 2, [dma((2,))]
    )
    passing = call("passing", passing_kernel, [array(n + tight, n)], middle, middle_z)
    passed = exchange(passing, "gx")
    (v0,), start0 = middles([0], 0, own_a, far_a)
    z0 = exchange(v0, "gy")
    half_z = copy(half_z, "relay")
    half_x = exchange(half_z, "gx")
    (v1,), start1 = middles([1], 0, own_a, far_a)
    z1 = exchange(v1, "gy")
    own_b, far_b = sides(bases[2], widths[2])
    known_b = known_half("known", known_kernel, 2, [], [], [])
    across_far, s_own, s_off, s_far = call(
        "build",
        build_kernel,
        [array(n, n)] * 4,
        middle,
        middle_z,
        passed,
        far_a,
        inverse1,
        half_z,
        half_x,
        across,
        scratch=[pltpu.VMEM((n, n), F32)],
    )
    own_c, far_c = sides(bases[3], 2 * unit)
    head, reach, rest = call("head", head_kernel, [array(h, h)] * 3, s_own)
    w0, w0_far = total(v0, z0, "opening")
    (v2,), start2 = middles([2], bases[2], own_b, far_b)
    z2 = exchange(v2, "gy")
    done, wide, left = call("turn", turn_kernel, [array(n, n)] * 3, head, reach, rest, s_off, s_far)
    w1, w1_far = total(v1, z1)
    (v3,), start3 = middles([3], bases[3], own_c, far_c)
    z3 = exchange(v3, "gy")
    head, reach, rest = call("head", head_kernel, [array(h, h)] * 3, left)
    w2, w2_far = total(v2, z2)
    inverse2 = call(
        "tail", tail_kernel, [array(2 * n, 2 * n, dtype=BF16)] * 2, head, reach, rest, done, wide, across, across_far
    )

    def last(base, own, far, starts, held):
        width = sum(part.shape[1] for part in own)
        fixed = 8 + 2 * len(own) + len(starts)
        return call(
            "last",
            functools.partial(last_kernel, len(own), base),
            [array(full, count), array(full, count)],
            *inverse2,
            *known_a,
            *known_b,
            *own,
            *far,
            *starts,
            *held[1:],
            *held[:1],
            ins=[WHOLE] * fixed + [ANY] * len(held),
            out_specs=[ANY] * 2,
            scratch=[pltpu.VMEM((2 * n, width), F32), pltpu.VMEM((full, width), F32), dma((6,))],
            aliases={fixed: 1, fixed + 1: 0},
        )

    w3, w3_far = total(v3, z3, "closing")
    w0_far = copy(w0_far)
    held = last(0, [w0, w1, w2], [w0_far, w1_far, w2_far], [start0, start1, start2], [flux, potential])
    held = last(bases[3], [w3], [w3_far], [start3], held)
    return held[1][None, None], held[0][None, None]


def solution(mesh):
    spec = P("gx", "gy", None, None)
    return jax.shard_map(per_device, mesh=mesh, in_specs=(spec, spec), out_specs=(spec, spec), check_vma=False)
```

```python
import functools

import jax
import jax.numpy as jnp
from jax import lax
from jax.experimental import pallas as pl
from jax.experimental.pallas import tpu as pltpu
from jax.sharding import PartitionSpec as P

HIGHEST = lax.Precision.HIGHEST
F32 = jnp.float32
BF16 = jnp.bfloat16
LANES = 128
PANEL = 8
TURN = 8


def exchange(block, axis):
    half = lax.axis_size(axis) // 2
    return lax.ppermute(block, axis, [(i, i ^ half) for i in range(2 * half)])


def side(axis):
    return (lax.axis_index(axis) >= lax.axis_size(axis) // 2).astype(jnp.int32)


def edges():
    c, r = side("gx"), side("gy")
    return 1 - c, c, 3 - r, 2 + r


def contract(left, right, dims):
    return lax.dot_general(left, right, ((dims[:1], dims[1:]), ((), ())), precision=HIGHEST, preferred_element_type=F32)


def full_nn(left, right):
    return contract(left, right, (1, 0))


def full_nt(left, right):
    return contract(left, right, (1, 1))


def full_tn(left, right):
    return contract(left, right, (0, 0))


def split(values):
    high = values.astype(BF16)
    return high, (values - high.astype(F32)).astype(BF16)


def half_dot(left, right):
    return jnp.dot(left, right, preferred_element_type=F32)


def triple(left, right):
    (lh, ll), (rh, rl) = left, right
    return half_dot(lh, rh) + (half_dot(lh, rl) + half_dot(ll, rh))


def near_nn(left, right):
    return triple(split(left), split(right))


def near_nt(left, right):
    return near_nn(left, right.T)


def near_tn(left, right):
    return near_nn(left.T, right)


def tree(terms):
    while len(terms) > 1:
        terms = [a + b for a, b in zip(terms[::2], terms[1::2])]
    return terms[0]


def entry(i, j):
    return (i, j) if i >= j else (j, i)


def invert_panel(s):
    s = dict(s)
    for k in range(PANEL):
        inverse = 1.0 / s[k, k]
        rest = [i for i in range(PANEL) if i != k]
        column = {i: s[entry(i, k)] for i in rest}
        scaled = {i: column[i] * inverse for i in rest}
        for i in rest:
            for j in rest:
                if j <= i:
                    s[i, j] = s[i, j] - scaled[i] * column[j]
        for i in rest:
            s[entry(i, k)] = scaled[i]
        s[k, k] = -inverse
    return {key: -value for key, value in s.items()}


def invert_tile(tile):
    shape = (PANEL, LANES)
    lane = lax.broadcasted_iota(jnp.int32, shape, 1)
    sub = lax.broadcasted_iota(jnp.int32, shape, 0)
    count = LANES // PANEL

    def turn(_, rows):
        rows = list(rows)
        for q in range(TURN):
            start = PANEL * q
            panel = rows[q]
            columns = [jnp.broadcast_to(panel[:, start + j : start + j + 1], shape) for j in range(PANEL)]
            s = {(i, j): jnp.broadcast_to(columns[j][i : i + 1, :], shape) for i in range(PANEL) for j in range(i + 1)}
            inverse = invert_panel(s)
            inside = (lane >= start) & (lane < start + PANEL)
            unit = jnp.where(inside, jnp.where(lane - start == sub, 1.0, 0.0), panel)
            wide = [jnp.broadcast_to(unit[j : j + 1, :], shape) for j in range(PANEL)]
            swept = [tree([inverse[entry(i, j)] * wide[j] for j in range(PANEL)]) for i in range(PANEL)]
            new = swept[0]
            for i in range(1, PANEL):
                new = jnp.where(sub == i, swept[i], new)
            for p in [*range(q + 1, count), *range(q)]:
                row = rows[p]
                terms = [jnp.broadcast_to(row[:, start + j : start + j + 1], shape) * swept[j] for j in range(PANEL)]
                rows[p] = jnp.where(inside, 0.0, row) - tree(terms)
            rows[q] = new
        return tuple(pltpu.roll(row, LANES - PANEL * TURN, 1) for row in rows[TURN:] + rows[:TURN])

    rows = tuple(tile[PANEL * i : PANEL * (i + 1), :] for i in range(count))
    return jnp.concatenate(lax.fori_loop(0, count // TURN, turn, rows), 0)


def invert(matrix):
    size = matrix.shape[0]
    if size == LANES:
        return invert_tile(matrix)
    half = size // 2
    first, cross, last = matrix[:half, :half], matrix[:half, half:], matrix[half:, half:]
    head = invert(first)
    reach = full_nn(head, cross)
    tail = invert(last - full_tn(cross, reach))
    return join(head, reach, tail)


def join(head, reach, tail):
    corner = full_nn(reach, tail)
    top = jnp.concatenate([head + full_nt(corner, reach), -corner], 1)
    return jnp.concatenate([top, jnp.concatenate([-corner.T, tail], 1)], 0)


def near_join(head, reach, tail):
    corner = near_nn(reach, tail)
    top = jnp.concatenate([head + near_nt(corner, reach), -corner], 1)
    return jnp.concatenate([top, jnp.concatenate([-corner.T, tail], 1)], 0)


def unpack(packed):
    h = packed.shape[1] // 2
    low = jnp.concatenate([packed[h:, :h], packed[h:, h:]], 0)
    return jnp.concatenate(
        [jnp.concatenate([packed[:h, :h], low.T], 1), jnp.concatenate([low, packed[:h, h:]], 1)], 0
    )


def fold(square):
    h = square.shape[0] // 2
    low = square[h:, :h]
    top = jnp.concatenate([square[:h, :h], square[h:, h:]], 1)
    return jnp.concatenate([top, jnp.concatenate([low[: h // 2], low[h // 2 :]], 1)], 0)


def fold_twice(square):
    h = square.shape[0] // 2
    once = fold(square)
    top = jnp.concatenate([fold(once[:h, :h]), fold(once[:h, h:])], 1)
    return jnp.concatenate([top, once[h:]], 0)


def unfold_twice(packed):
    h = packed.shape[1] // 2
    tall = 3 * h // 4
    top = jnp.concatenate([unpack(packed[:tall, :h]), unpack(packed[:tall, h:])], 1)
    return unpack(jnp.concatenate([top, packed[tall:]], 0))


def quarters(leaf, n, a, b):
    h = n // 2

    def block(row, rows, col):
        return leaf.at[pl.ds(pl.multiple_of(a * n + row, h // 2), rows), pl.ds(pl.multiple_of(b * n + col, h), h)]

    return block


def fetch(moves, sems):
    copies = [pltpu.make_async_copy(a, b, sems.at[k]) for k, (a, b) in enumerate(moves)]
    for copy in copies:
        copy.start()
    for copy in copies:
        copy.wait()


def symmetric(leaf, e, out, base):
    n = out.shape[1]
    h = n // 2
    block = quarters(leaf, n, e, e)
    return [
        (block(0, h, 0), out.at[pl.ds(base, h), pl.ds(0, h)]),
        (block(h, h, h), out.at[pl.ds(base, h), pl.ds(h, h)]),
        (block(h, h // 2, 0), out.at[pl.ds(base + h, h // 2), pl.ds(0, h)]),
        (block(h + h // 2, h // 2, 0), out.at[pl.ds(base + h, h // 2), pl.ds(h, h)]),
    ]


def blocks_kernel(leaf, joined, middle, held, sems):
    n = joined.shape[1]
    i, _, y, _ = edges()
    block = lambda a, b: leaf.at[pl.ds(pl.multiple_of(a * n, n), n), pl.ds(pl.multiple_of(b * n, n), n)]
    fetch([(block(y, y), held), (block(y, i), middle.at[pl.ds(0, n)])] + symmetric(leaf, i, joined, 0), sems)
    middle[n:] = fold_twice(held[...])


def passing_kernel(middle, middle_z, out):
    n = out.shape[1]
    out[:n] = middle_z[:n]
    out[n:] = middle[n:] + middle_z[n:]


def relay_kernel(given, out):
    out[...] = given[...]


def sum_kernel(own, other, out):
    out[...] = own[...] + other[...]


def outer_rows(leaf, edge, rows, sems):
    n = rows.shape[0]
    _, x, _, d = edges()
    own = pl.ds(pl.multiple_of(edge * n, n), n)
    return [
        pltpu.make_async_copy(leaf.at[own, pl.ds(pl.multiple_of(e * n, n), n)], rows.at[:, pl.ds(p * n, n)], sems.at[p])
        for p, e in enumerate((x, d))
    ]


def side_kernel(base, leaf, data, out, rows, held, sems):
    n, width = rows.shape[0], held.shape[1]
    i, _, y, _ = edges()
    copies = outer_rows(leaf, i, rows, sems)
    copies.append(pltpu.make_async_copy(data.at[:, pl.ds(base, width)], held, sems.at[2]))
    for copy in copies:
        copy.start()
    if out.shape[1] > width:
        whole = leaf.at[pl.ds(pl.multiple_of(y * n, n), n), pl.ds(pl.multiple_of(i * n, n), n)]
        fetch([(whole, out.at[:, pl.ds(width, n)])], sems.at[pl.ds(3, 1)])
    for copy in copies:
        copy.wait()
    out[:, :width] = triple(split(rows[...]), split(held[...]))


def known_kernel(leaf, data, flux, high, low, data_high, data_low):
    n = leaf.shape[0]
    i, x, y, d = edges()

    @pl.when(pl.program_id(0) == 0)
    def _():
        data_high[...], data_low[...] = split(data[...])

    cols = lambda e: leaf[:, pl.ds(pl.multiple_of(e * n, n), n)]
    high[...], low[...] = split(jnp.concatenate([cols(i), cols(y)], 1))
    outer = split(jnp.concatenate([cols(x), cols(d)], 1))
    flux[...] = triple(outer, (data_high[...], data_low[...]))


def known_and_data_kernel(leaf, data, flux, high, low, potential, _, data_high, data_low, sems):
    n = leaf.shape[0]
    _, x, _, d = edges()
    copies = [
        pltpu.make_async_copy(data.at[pl.ds(p * n, n), :], potential.at[pl.ds(pl.multiple_of(e * n, n), n), :], sems.at[p])
        for p, e in enumerate((x, d))
    ]

    @pl.when(pl.program_id(0) == 0)
    def _():
        for copy in copies:
            copy.start()

    known_kernel(leaf, data, flux, high, low, data_high, data_low)

    @pl.when(pl.program_id(0) == pl.num_programs(0) - 1)
    def _():
        for copy in copies:
            copy.wait()


def first_kernel(joined, joined_far, middle, inverse, across, half):
    n = inverse.shape[0]
    h = n // 2
    solved = invert(unpack(joined[...] + joined_far[...]))
    inverse[...] = solved
    across[...] = near_nt(solved, middle[:n])

    def fill(diagonal, low):
        half[:h] = diagonal
        half[h:] = low

    @pl.when(side("gx") == 0)
    def _():
        fill(solved[:h, :h], solved[h : h + h // 2, :h])

    @pl.when(side("gx") == 1)
    def _():
        fill(solved[h:, h:], solved[h + h // 2 :, :h])


def middle_kernel(base, offset, widths, leaf, data, own, far, across, inverse, *rest):
    outs, (start, rows, held, sems) = rest[:-4], rest[-4:]
    width = sum(widths)
    copies = outer_rows(leaf, edges()[2], rows, sems)
    copies.append(pltpu.make_async_copy(data.at[:, pl.ds(base, width)], held, sems.at[2]))
    for copy in copies:
        copy.start()
    right = split(own[:, offset : offset + width] + far[:, offset : offset + width])
    start[...] = -triple(split(inverse[...]), right)
    out = triple(split(across[...].T), right)
    for copy in copies:
        copy.wait()
    out = triple(split(rows[...]), split(held[...])) - out
    done = 0
    for ref, part in zip(outs, widths):
        ref[...] = out[:, done : done + part]
        done += part


def build_kernel(middle, middle_z, passed, side_far, inverse, half_z, half_x, across, across_far, own, off, far, other):
    n = inverse.shape[0]
    h = n // 2

    def fill(one, two):
        low = jnp.concatenate([one[h:], two[h:]], 0)
        other[:h, :h] = one[:h]
        other[h:, h:] = two[:h]
        other[h:, :h] = low
        other[:h, h:] = low.T

    @pl.when(side("gx") == 0)
    def _():
        fill(half_z, half_x)

    @pl.when(side("gx") == 1)
    def _():
        fill(half_x, half_z)

    cross = side_far[:, -n:]
    q_far = near_nt(inverse[...], cross)
    q_own = across[...]
    across_far[...] = q_far
    p_own = near_nt(other[...], middle_z[:n])
    p_far = near_nt(other[...], passed[:n])
    own[...] = unfold_twice(middle[n:] + middle_z[n:]) - (near_nn(middle[:n], q_own) + near_nn(middle_z[:n], p_own))
    off[...] = -(near_nn(middle[:n], q_far) + near_nn(middle_z[:n], p_far))
    far[...] = unfold_twice(passed[n:]) - (near_nn(cross, q_far) + near_nn(passed[:n], p_far))


def open_half(matrix, head, reach, rest):
    h = matrix.shape[0] // 2
    solved = invert(matrix[:h, :h])
    head[...] = solved
    reach[...] = full_nn(solved, matrix[:h, h:])
    rest[...] = matrix[h:, h:] - full_tn(matrix[:h, h:], reach[...])


def head_kernel(matrix, head, reach, rest):
    open_half(matrix, head, reach, rest)


def turn_kernel(head, reach, rest, off, far, done, wide, left):
    done[...] = join(head[...], reach[...], invert(rest[...]))
    wide[...] = near_nn(done[...], off[...])
    left[...] = far[...] - near_tn(off[...], wide[...])


def tail_kernel(head, reach, rest, done, wide, across, across_far, high, low):
    n = done.shape[0]
    solved = near_join(done[...], wide[...], join(head[...], reach[...], invert(rest[...])))
    inward = triple(split(jnp.concatenate([across[...], across_far[...]], 1)), split(solved))
    high[...], low[...] = split(jnp.concatenate([inward, -solved[:n]], 0))


def last_kernel(count, base, solve_high, solve_low, *rest):
    halves, rest = (rest[:3], rest[3:6]), rest[6:]
    w_own, w_far, starts = rest[:count], rest[count : 2 * count], rest[2 * count : -7]
    flux, potential, solved, made, sems = rest[-5:]
    n, width = w_own[0].shape[0], solved.shape[1]
    i, _, y, _ = edges()
    cols = pl.ds(base, width)
    tops, rests, done = [], [], 0
    shift = jnp.concatenate([start[...] for start in starts], 1)
    for own, far in zip(w_own, w_far):
        part = slice(done, done + own.shape[1])
        inner = triple((solve_high[...], solve_low[...]), split(jnp.concatenate([own[...], far[...]], 0)))
        tops.append(inner[:n] + shift[:, part])
        rests.append(inner[n:])
        done = part.stop
    values = jnp.concatenate([jnp.concatenate(tops, 1), jnp.concatenate(rests, 1)], 0)
    solved[...] = values
    copies = []
    for p, e in enumerate((i, y)):
        rows = pl.ds(pl.multiple_of(e * n, n), n)
        copies.append(pltpu.make_async_copy(solved.at[pl.ds(p * n, n), :], potential.at[rows, cols], sems.at[4 + p]))
        copies[-1].start()
    right = split(values)
    for k in range(4):
        rows = pl.ds(k * n, n)
        known, high, low = (ref.at[pl.ds(k % 2 * n, n)] for ref in halves[k // 2])
        made[rows] = known[:, base : base + width] + triple((high[...], low[...]), right)
        copies.append(pltpu.make_async_copy(made.at[rows], flux.at[rows, cols], sems.at[k]))
        copies[-1].start()
    for copy in copies:
        copy.wait()


def array(*shape, dtype=F32):
    return jax.ShapeDtypeStruct(shape, dtype)


ANY = pl.BlockSpec(memory_space=pl.ANY)
HBM = pl.BlockSpec(memory_space=pltpu.HBM)
WHOLE = pl.BlockSpec(memory_space=pltpu.VMEM)
MIB = 1 << 20
EARLY = 58


COSTS = {
    "passing": 8.0,
    "relay": 8.0,
    "build": 0.7,
    "opening": 1.2,
    "copy": 0.05,
    "closing": 0.3,
}


class Chain:
    def __init__(self):
        self.mark = None

    def __call__(self, name, kernel, outs, *args, ins=None, out_specs=None, scratch=(), aliases=None, limit=24, **kwargs):
        cost = COSTS.get(name, 0.005)
        ins = ins or [WHOLE] * len(args)
        out_specs = out_specs or [WHOLE] * len(outs)
        marks = [] if self.mark is None else [self.mark]

        def body(*refs):
            inner = refs[: len(args)] + refs[len(args) + len(marks) :]
            kernel(*inner[: len(args) + len(outs)], *inner[len(args) + len(outs) + 1 :])

        *given, self.mark = pl.pallas_call(
            body,
            out_shape=list(outs) + [array(8, LANES)],
            in_specs=list(ins) + [HBM] * len(marks),
            out_specs=list(out_specs) + [HBM],
            scratch_shapes=list(scratch),
            input_output_aliases=aliases or {},
            compiler_params=pltpu.CompilerParams(vmem_limit_bytes=limit * MIB),
            cost_estimate=pl.CostEstimate(flops=int(cost * 1e9), bytes_accessed=int(cost * 3e6), transcendentals=0),
            name=name,
            **kwargs,
        )(*args, *marks)
        return given[0] if len(given) == 1 else given


def per_device(leaf_maps, edge_data):
    leaf = leaf_maps[0, 0]
    data = edge_data[0, 0]
    full, count = leaf.shape[0], data.shape[1]
    n = full // 4
    h = n // 2
    packed = 3 * n // 4
    tight = 5 * n // 8
    dma = pltpu.SemaphoreType.DMA
    call = Chain()
    unit = count // 8
    widths = [2 * unit] * 4
    bases = [0, 2 * unit, 4 * unit, 6 * unit]

    joined, middle = call(
        "blocks",
        blocks_kernel,
        [array(packed, n), array(n + tight, n)],
        leaf,
        limit=EARLY,
        ins=[HBM],
        scratch=[pltpu.VMEM((n, n), F32), dma((6,))],
    )
    middle_z = exchange(middle, "gy")
    joined_far = exchange(joined, "gx")

    def sides(base, width, extra=0):
        own = call(
            "side",
            functools.partial(side_kernel, base),
            [array(n, width + extra)],
            leaf,
            data,
            ins=[HBM] * 2,
            scratch=[pltpu.VMEM((n, 2 * n), F32), pltpu.VMEM((2 * n, width), F32), dma((4,))],
        )
        return own, exchange(own, "gx")

    def middles(parts, offset, own, far):
        base, width = bases[parts[0]], sum(widths[k] for k in parts)
        given = call(
            "middle",
            functools.partial(middle_kernel, base, base - offset, [widths[k] for k in parts]),
            [array(n, widths[k]) for k in parts] + [array(n, width)],
            leaf,
            data,
            own,
            far,
            across,
            inverse1,
            ins=[ANY] * 2 + [WHOLE] * 4,
            scratch=[pltpu.VMEM((n, 2 * n), F32), pltpu.VMEM((2 * n, width), F32), dma((3,))],
        )
        return given[:-1], given[-1]

    def total(own, far, name="total"):
        w = call(name, sum_kernel, [array(*own.shape)], own, far)
        return w, exchange(w, "gx")

    def copy(given, name="copy"):
        return call(name, relay_kernel, [array(*given.shape)], given)

    own_a, far_a = sides(0, 4 * unit, n)
    inverse1, across, half = call(
        "first", first_kernel, [array(n, n)] * 2 + [array(packed, h)], joined, joined_far, middle
    )
    half_z = exchange(half, "gy")
    def known_half(name, kernel, first, outs, out_specs, sems):
        return call(
            name,
            kernel,
            [array(2 * n, count), array(2 * n, 2 * n, dtype=BF16), array(2 * n, 2 * n, dtype=BF16), *outs],
            leaf,
            data,
            ins=[pl.BlockSpec((n, full), lambda s: (s + first, 0)), pl.BlockSpec((2 * n, count), lambda s: (0, 0))],
            out_specs=[
                pl.BlockSpec((n, count), lambda s: (s, 0)),
                pl.BlockSpec((n, 2 * n), lambda s: (s, 0)),
                pl.BlockSpec((n, 2 * n), lambda s: (s, 0)),
                *out_specs,
            ],
            scratch=[pltpu.VMEM((2 * n, count), BF16), pltpu.VMEM((2 * n, count), BF16), *sems],
            grid=(2,),
        )

    *known_a, potential, flux = known_half(
        "known_and_data", known_and_data_kernel, 0, [array(full, count)] * 2, [ANY] * 2, [dma((2,))]
    )
    passing = call("passing", passing_kernel, [array(n + tight, n)], middle, middle_z)
    passed = exchange(passing, "gx")
    (v0,), start0 = middles([0], 0, own_a, far_a)
    z0 = exchange(v0, "gy")
    half_z = copy(half_z, "relay")
    half_x = exchange(half_z, "gx")
    (v1,), start1 = middles([1], 0, own_a, far_a)
    z1 = exchange(v1, "gy")
    own_b, far_b = sides(bases[2], widths[2])
    own_c, far_c = sides(bases[3], 2 * unit)
    known_b = known_half("known", known_kernel, 2, [], [], [])
    across_far, s_own, s_off, s_far = call(
        "build",
        build_kernel,
        [array(n, n)] * 4,
        middle,
        middle_z,
        passed,
        far_a,
        inverse1,
        half_z,
        half_x,
        across,
        scratch=[pltpu.VMEM((n, n), F32)],
    )
    head, reach, rest = call("head", head_kernel, [array(h, h)] * 3, s_own)
    w0, w0_far = total(v0, z0, "opening")
    (v2,), start2 = middles([2], bases[2], own_b, far_b)
    z2 = exchange(v2, "gy")
    done, wide, left = call("turn", turn_kernel, [array(n, n)] * 3, head, reach, rest, s_off, s_far)
    w1, w1_far = total(v1, z1)
    (v3,), start3 = middles([3], bases[3], own_c, far_c)
    z3 = exchange(v3, "gy")
    head, reach, rest = call("head", head_kernel, [array(h, h)] * 3, left)
    w2, w2_far = total(v2, z2)
    inverse2 = call(
        "tail", tail_kernel, [array(2 * n, 2 * n, dtype=BF16)] * 2, head, reach, rest, done, wide, across, across_far
    )

    def last(base, own, far, starts, held):
        width = sum(part.shape[1] for part in own)
        fixed = 8 + 2 * len(own) + len(starts)
        return call(
            "last",
            functools.partial(last_kernel, len(own), base),
            [array(full, count), array(full, count)],
            *inverse2,
            *known_a,
            *known_b,
            *own,
            *far,
            *starts,
            *held[1:],
            *held[:1],
            ins=[WHOLE] * fixed + [ANY] * len(held),
            out_specs=[ANY] * 2,
            scratch=[pltpu.VMEM((2 * n, width), F32), pltpu.VMEM((full, width), F32), dma((6,))],
            aliases={fixed: 1, fixed + 1: 0},
        )

    w3, w3_far = total(v3, z3, "closing")
    w0_far = copy(w0_far)
    held = last(0, [w0, w1, w2], [w0_far, w1_far, w2_far], [start0, start1, start2], [flux, potential])
    held = last(bases[3], [w3], [w3_far], [start3], held)
    return held[1][None, None], held[0][None, None]


def solution(mesh):
    spec = P("gx", "gy", None, None)
    return jax.shard_map(per_device, mesh=mesh, in_specs=(spec, spec), out_specs=(spec, spec), check_vma=False)
```
